32 devices in a mesh: expert: 4 (over y, x), tensor: 8 (over z, core).
Axes of the slice: x: 2, y: 2, z: 4, core: 2. Of those that a mesh axis runs over, the one named last changes fastest.
Arguments:
- queries: bfloat16 [512, 8192], P('expert', 'tensor'), may hold values from -8 to 8
- keys_values: bfloat16 [4, 4, 1152, 256], P('expert'), may hold values from -6 to 6
- prefix_len: int32 [4], P('expert'), may hold values from 128 to 1024, as said below
- out_proj: bfloat16 [8192, 4096], P('tensor', 'expert'), may hold values from -0.0625 to 0.0625
- residual: bfloat16 [512, 4096], P(('expert', 'tensor')), may hold values from -1.796875 to 1.796875
- norm_gain: float32 [4096], replicated, may hold values from 0.1 to 1.9
- expert_ids: int32 [512, 8], P('expert'), may hold values from 0 to 7, all different within a row; in each aligned block of 16 rows (0 to 15, 16 to 31, ...) at most 16 rows name the same one
- route_weights: bfloat16 [512, 8], P('expert'), may hold values from 0.19921875 to 1
- w_gate: bfloat16 [32, 4096, 384], P(('expert', 'tensor')), may hold values from -0.09375 to 0.09375
- w_up: bfloat16 [32, 4096, 384], P(('expert', 'tensor')), may hold values from -0.09375 to 0.09375
- w_down: bfloat16 [32, 384, 4096], P(('expert', 'tensor')), may hold values from -0.15625 to 0.15625
Outputs:
- layer_out: bfloat16 [512, 4096], P(('expert', 'tensor'))
The draws below stay inside these ranges and needn't reach their ends.
Inputs may be any that keep to these rules, and one draw needn't show every extreme that they name: `expert_ids`: in the rows of one device (aligned blocks of 16 rows) no expert is named by more than 16 rows, a bound that some block reaches; a row names 8 different experts. `prefix_len`: some sequence has all 1024 slots live.
All inputs are finite; a program needn't handle non-finite values.
Results may differ from the reference program's by a relative error of at most 0.035.
Values may be sent and summed in bfloat16 or wider, within the bound.
A program may use at most 128 MiB of HBM per device.

```python
import math
import jax
import jax.numpy as jnp
import numpy as np
from jax import lax

D = 4096
HEADS = 64
KVH = 4
HD = 128
FFE = 1536
TOPK = 8
HSPLIT = 4
TOK_DEV = 16
PREFIX = 1024
EXPERTS = 8
QH = 384
STEP_TOKENS = 128
CTX = 1152
TOKENS = 512
MOST = 16
CAP = 128
N_EXPERT = 4
N_TENSOR = 8


def attention_pair(key):
    joint = jax.random.fold_in(key, 11)
    first_key, second_key = jax.random.split(joint, 2)
    query_all = jnp.clip(2.0 * jax.random.normal(first_key, (N_EXPERT * STEP_TOKENS, HEADS * HD), jnp.float32), -8.0, 8.0)
    cached = jnp.clip(jax.random.normal(second_key, (N_EXPERT, KVH, CTX, 2 * HD), jnp.float32), -6.0, 6.0)
    return (query_all, cached)


def draw_queries(key, part):
    return attention_pair(key)[0].astype(jnp.bfloat16)


def draw_keys_values(key, part):
    return attention_pair(key)[1].astype(jnp.bfloat16)


def draw_prefix_len(key, part):
    length_key, pick_key = jax.random.split(jax.random.fold_in(key, 23))
    lengths = jax.random.randint(length_key, (N_EXPERT,), PREFIX // 8, PREFIX + 1)
    longest = jax.random.randint(pick_key, (), 0, N_EXPERT)
    return jnp.where(jnp.arange(N_EXPERT) == longest, PREFIX, lengths).astype(jnp.int32)


def block_levels(own_key, dims, pieces, smallest, top_value):
    factor_of, own = 1.0, jax.random.fold_in(own_key, 6)
    for position, parts in pieces:
        heights = jnp.exp(jax.random.uniform(jax.random.fold_in(own, position), (parts,), jnp.float32, smallest / len(pieces), top_value / len(pieces)))
        factor_of = factor_of * jnp.repeat(heights, dims[position] // parts).reshape([-1 if axis == position else 1 for axis in range(len(dims))])
    return factor_of


def assign_block(own_key, own, number, rows, amount, top, reach, lean):
    ranking = jax.random.permutation(own_key, amount)
    crowded, ordinary = portions_of(amount, rows * top, reach, lean, True), portions_of(amount, rows * top, reach, lean, False)
    places = jnp.arange(amount)

    def named(sizes, offset_by):
        used = int((sizes > 0).sum())
        fixed = max(1, used // 4)
        shifted = fixed + (places - fixed + offset_by * (used - fixed)) % max(1, amount - fixed)
        return jnp.zeros((amount,), jnp.int32).at[ranking[jnp.where(places < fixed, places, shifted)]].set(jnp.asarray(sizes, jnp.int32))

    sizes = jnp.where(number % 4 == 0, named(crowded, number // 4), named(ordinary, number - number // 4 - 1))
    mixed = jax.random.permutation(jax.random.fold_in(own, 3), amount)
    giver, sink = mixed[0:amount // 2 * 2:2], mixed[1:amount // 2 * 2:2]
    room = jnp.minimum(sizes[giver] - 1, reach - sizes[sink]) // 2
    room = jnp.where((giver == ranking[0]) | (sink == ranking[0]) | (sizes[sink] == 0), 0, jnp.maximum(room, 0))
    shifted = jax.random.randint(jax.random.fold_in(own, 4), (amount // 2,), 0, 1 << 20) % (room + 1)
    sizes = sizes.at[giver].add(-shifted).at[sink].add(shifted)
    members = jnp.searchsorted(jnp.cumsum(sizes), jnp.arange(rows * top), side="right").astype(jnp.int32)
    listing = members.reshape(top, rows).T
    listing = listing[jax.random.permutation(jax.random.fold_in(own, 1), rows)]
    offset_by = jax.random.randint(jax.random.fold_in(own, 2), (rows, 1), 0, top)
    return jnp.take_along_axis(listing, (jnp.arange(top)[None, :] + offset_by) % top, axis=1)


def portions_of(count, total, reach, lean, full):
    loads = [(1 << 20) // math.isqrt(standing ** lean) + 1 for standing in range(1, count + 1)]
    largest = reach if full else min(reach, max(-(-total // count), total * loads[0] // sum(loads)))
    least = 1 if total - largest >= count - 1 else 0
    counts, spare = [largest] + [least] * (count - 1), total - largest - least * (count - 1)
    while spare > 0:
        movable = [i for i in range(1, count) if counts[i] < largest] or [i for i in range(1, count) if counts[i] < reach]
        whole, remaining = sum([loads[i] for i in movable]), spare
        for i in movable:
            more = min(reach - counts[i], max(1, remaining * loads[i] // whole), spare)
            counts[i] = counts[i] + more
            spare = spare - more
    return np.array(counts)


def scatter_about(stream_key, shape, spread, reach, shards=(), kind=jnp.bfloat16):
    factor_of = block_levels(stream_key, shape, shards, -0.22, 0.18) if shards else 1.0
    values = jax.random.normal(stream_key, shape, jnp.float32) * spread * factor_of
    return jnp.minimum(jnp.maximum(values, -reach), reach).astype(kind)


def setup_inputs(seed: int = 0) -> dict:
    key_list = jax.random.split(jax.random.key(seed), 12)
    queries = draw_queries(jax.random.fold_in(key_list[11], 71), 0)
    keys_values = draw_keys_values(jax.random.fold_in(key_list[11], 71), 0)
    prefix_len = draw_prefix_len(jax.random.fold_in(key_list[11], 71), 0)
    out_proj = scatter_about(key_list[3], (HEADS * HD, D), (HEADS * HD) ** -0.5, 0.0625, ((0, 8), (1, 4)))
    residual = scatter_about(key_list[4], (TOKENS, D), 0.3, 1.796875, ((0, 32),))
    norm_gain = jnp.clip(1.0 + 0.18 * jax.random.normal(key_list[5], (D,), jnp.float32), 0.1, 1.9)
    expert_ids_keys = jax.random.split(jax.random.fold_in(key_list[6], 1), TOKENS // TOK_DEV)
    expert_ids_turns = jax.random.permutation(jax.random.fold_in(key_list[6], 3), TOKENS // TOK_DEV)
    expert_ids = jax.vmap(lambda own, number: assign_block(jax.random.fold_in(key_list[6], 2), own, number, TOK_DEV, EXPERTS, TOPK, MOST, 2))(expert_ids_keys, expert_ids_turns).reshape((TOKENS, TOPK))
    route_weights = jnp.clip(0.19921875 + 0.80078125 * jax.random.uniform(key_list[7], (TOKENS, TOPK), jnp.float32) ** block_levels(key_list[7], (TOKENS, TOPK), ((0, 4),), -0.2, 0.2), 0.19921875, 1.0).astype(jnp.bfloat16)
    w_gate = scatter_about(key_list[8], (EXPERTS * HSPLIT, D, QH), D ** -0.5, 0.09375, ((0, 32),))
    w_up = scatter_about(key_list[9], (EXPERTS * HSPLIT, D, QH), D ** -0.5, 0.09375, ((0, 32),))
    w_down = scatter_about(key_list[10], (EXPERTS * HSPLIT, QH, D), FFE ** -0.5, 0.15625, ((0, 32),))
    return {"queries": queries, "keys_values": keys_values, "prefix_len": prefix_len, "out_proj": out_proj, "residual": residual, "norm_gain": norm_gain, "expert_ids": expert_ids, "route_weights": route_weights, "w_gate": w_gate, "w_up": w_up, "w_down": w_down}


def reference(queries, keys_values, prefix_len, out_proj, residual, norm_gain, expert_ids, route_weights, w_gate, w_up, w_down):
    group_size = HEADS // KVH
    per_device = HEADS // N_TENSOR
    projection = out_proj.astype(jnp.float32).reshape(N_TENSOR, per_device * HD, D)

    def one_sequence(sequence):
        query_rows = lax.dynamic_slice_in_dim(queries, sequence * STEP_TOKENS, STEP_TOKENS, 0).astype(jnp.float32)
        query_rows = query_rows.reshape(STEP_TOKENS, KVH, group_size, HD)
        cached = lax.dynamic_index_in_dim(keys_values, sequence, 0, keepdims=False).astype(jnp.float32)
        key_rows = cached[:, :, :HD]
        value_rows = cached[:, :, HD:]
        scores = jnp.einsum('ngqd,gcd->gqnc', query_rows, key_rows) / math.sqrt(HD)
        length = lax.dynamic_index_in_dim(prefix_len, sequence, 0, keepdims=False)
        columns = jnp.arange(CTX, dtype=jnp.int32)[None, :]
        positions = jnp.arange(STEP_TOKENS, dtype=jnp.int32)[:, None]
        visible = ((columns < length) | (columns >= PREFIX) & (columns - PREFIX <= positions))[None, None]
        highest = lax.optimization_barrier(jnp.max(jnp.where(visible, scores, -1e+30), axis=-1, keepdims=True))
        weights = jnp.exp(jnp.where(visible, scores - highest, -1e+30))
        summed = lax.optimization_barrier(jnp.sum(weights, axis=-1))
        rounded = lax.optimization_barrier(weights.astype(jnp.bfloat16)).astype(jnp.float32)
        blended = jnp.einsum('gqnc,gcd->ngqd', rounded, value_rows)
        blended = blended / jnp.transpose(summed, (2, 0, 1))[:, :, :, None]
        attended = blended.reshape(STEP_TOKENS, HEADS * HD).astype(jnp.bfloat16)
        head_parts = jnp.einsum('ntk,tkd->tnd', attended.astype(jnp.float32).reshape(STEP_TOKENS, N_TENSOR, per_device * HD), projection)
        head_parts = lax.optimization_barrier(head_parts.astype(jnp.bfloat16)).astype(jnp.float32)
        rows_in = lax.dynamic_slice_in_dim(residual, sequence * STEP_TOKENS, STEP_TOKENS, 0).astype(jnp.float32)
        return (rows_in + lax.optimization_barrier(jnp.sum(head_parts, axis=0))).astype(jnp.bfloat16)
    hidden_state = lax.map(one_sequence, jnp.arange(N_EXPERT, dtype=jnp.int32)).reshape(TOKENS, D)
    values = hidden_state.astype(jnp.float32)
    normed = values * lax.rsqrt(lax.optimization_barrier(jnp.mean(values * values, axis=-1, keepdims=True)) + 1e-06) * norm_gain[None, :]
    normed = normed.astype(jnp.bfloat16)
    row_ids = jnp.arange(TOKENS, dtype=jnp.int32)
    named_mask = expert_ids[:, :, None] == jnp.arange(EXPERTS, dtype=jnp.int32)[None, None, :]
    hit_table = lax.optimization_barrier(jnp.sum(named_mask.astype(jnp.int32), axis=1)).astype(jnp.int32)
    weight_table = lax.optimization_barrier(jnp.sum(jnp.where(named_mask, route_weights[:, :, None].astype(jnp.float32), 0.0), axis=1))
    grouped = hit_table.reshape(TOKENS // TOK_DEV, TOK_DEV, EXPERTS)
    rank_table = (jnp.cumsum(grouped, axis=1) - grouped).reshape(TOKENS, EXPERTS).astype(jnp.int32)
    slot_column = ((row_ids // STEP_TOKENS)[:, None] * CAP + (row_ids // TOK_DEV % N_TENSOR)[:, None] * MOST + rank_table).astype(jnp.int32)
    expert_column = jnp.where(hit_table == 1, jnp.arange(EXPERTS, dtype=jnp.int32)[None, :], EXPERTS).astype(jnp.int32)
    source_table = jnp.full((EXPERTS, N_EXPERT * CAP), TOKENS, jnp.int32)
    source_table = source_table.at[expert_column.reshape(-1), slot_column.reshape(-1)].set(jnp.broadcast_to(row_ids[:, None], (TOKENS, EXPERTS)).reshape(-1), mode='drop')
    gain_table = jnp.zeros((EXPERTS, N_EXPERT * CAP), jnp.float32)
    gain_table = gain_table.at[expert_column.reshape(-1), slot_column.reshape(-1)].set(weight_table.reshape(-1), mode='drop')

    def one_expert(accumulated, expert):
        expert = expert.astype(jnp.int32)
        sources = lax.dynamic_index_in_dim(source_table, expert, 0, keepdims=False)
        gain_row = lax.dynamic_index_in_dim(gain_table, expert, 0, keepdims=False)
        inputs = jnp.take(normed, jnp.minimum(sources, TOKENS - 1), axis=0)
        total = jnp.zeros((N_EXPERT * CAP, D), jnp.float32)
        for quarter in range(HSPLIT):
            weight_row = (expert * HSPLIT + quarter).astype(jnp.int32)
            gate_w = lax.dynamic_index_in_dim(w_gate, weight_row, 0, keepdims=False)
            up_w = lax.dynamic_index_in_dim(w_up, weight_row, 0, keepdims=False)
            down_w = lax.dynamic_index_in_dim(w_down, weight_row, 0, keepdims=False)
            gate_val = jnp.dot(inputs, gate_w, preferred_element_type=jnp.float32)
            up_val = jnp.dot(inputs, up_w, preferred_element_type=jnp.float32)
            inner = (jax.nn.silu(gate_val) * up_val).astype(jnp.bfloat16)
            result = jnp.dot(inner, down_w, preferred_element_type=jnp.float32).astype(jnp.bfloat16)
            result = lax.optimization_barrier(result).astype(jnp.float32)
            total = total + gain_row[:, None] * result
        accumulated = accumulated.at[sources].add(total, mode='drop')
        return (accumulated, None)
    expert_sum, _ = lax.scan(one_expert, jnp.zeros((TOKENS, D), jnp.float32), jnp.arange(EXPERTS, dtype=jnp.int32))
    return (hidden_state.astype(jnp.float32) + expert_sum).astype(jnp.bfloat16)
```

```python
import math

import jax
import jax.numpy as jnp
from jax import lax
from jax.sharding import PartitionSpec as P

HEADS = 64
KVH = 4
HD = 128
TOPK = 8
HSPLIT = 4
TOK_DEV = 16
PREFIX = 1024


def norm_rows(hidden_state, norm_gain):
    values = hidden_state.astype(jnp.float32)
    factor = lax.rsqrt(jnp.mean(values * values, axis=-1, keepdims=True) + 1e-06)
    return (values * factor * norm_gain[None, :]).astype(jnp.bfloat16)


def route_tables(expert_ids, route_weights, experts, most_rows):
    total_rows = expert_ids.shape[0]
    named_mask = expert_ids[:, :, None] == jnp.arange(experts, dtype=jnp.int32)[None, None, :]
    hit_table = jnp.sum(named_mask.astype(jnp.int32), axis=1)
    weight_table = jnp.sum(
        jnp.where(named_mask, route_weights[:, :, None].astype(jnp.float32), 0.0), axis=1
    )
    grouped = hit_table.reshape(total_rows // TOK_DEV, TOK_DEV, experts)
    rank_table = (jnp.cumsum(grouped, axis=1) - grouped).reshape(total_rows, experts)
    share_index = (jnp.arange(total_rows, dtype=jnp.int32) // TOK_DEV)[:, None]
    position_table = share_index * most_rows + rank_table
    return (hit_table, weight_table, rank_table, position_table)


def pick_slot(table, expert_count, slot_count, slot_index):
    shaped = table.reshape(table.shape[0], expert_count, slot_count)
    return lax.dynamic_index_in_dim(shaped, slot_index, 2, keepdims=False)


def shards(
    queries,
    keys_values,
    prefix_len,
    out_proj,
    residual,
    norm_gain,
    expert_ids,
    route_weights,
    w_gate,
    w_up,
    w_down,
):
    tensor_count = lax.axis_size("tensor")
    expert_count = lax.axis_size("expert")
    tensor_index = lax.axis_index("tensor")
    step_rows = queries.shape[0]
    per_device = queries.shape[1] // HD
    group_size = HEADS // KVH
    kv_index = tensor_index * per_device // group_size
    cached = lax.dynamic_index_in_dim(keys_values[0], kv_index, 0, keepdims=False)
    key_rows = cached[:, :HD]
    value_rows = cached[:, HD:]
    context = cached.shape[0]
    query_rows = queries.reshape(step_rows, per_device, HD)
    scores = jnp.einsum(
        "nhd,cd->hnc", query_rows, key_rows, preferred_element_type=jnp.float32
    ) / math.sqrt(HD)
    columns = jnp.arange(context, dtype=jnp.int32)[None, :]
    positions = jnp.arange(step_rows, dtype=jnp.int32)[:, None]
    visible = ((columns < prefix_len[0]) | (columns >= PREFIX) & (columns - PREFIX <= positions))[
        None
    ]
    highest = jnp.max(jnp.where(visible, scores, -1e30), axis=-1, keepdims=True)
    weights = jnp.exp(jnp.where(visible, scores - highest, -1e30))
    summed = jnp.sum(weights, axis=-1)
    blended = jnp.einsum(
        "hnc,cd->nhd", weights.astype(jnp.bfloat16), value_rows, preferred_element_type=jnp.float32
    )
    attended = (
        (blended / jnp.transpose(summed)[:, :, None])
        .astype(jnp.bfloat16)
        .reshape(step_rows, per_device * HD)
    )
    head_part = jnp.dot(
        attended,
        lax.all_gather(out_proj, "expert", axis=1, tiled=True),
        preferred_element_type=jnp.float32,
    )
    slot_count = tensor_count // HSPLIT
    experts = expert_count * slot_count
    most_rows = min(TOK_DEV, max(2, TOK_DEV * TOPK // experts + 1))
    capacity = tensor_count * most_rows
    slot_index = tensor_index // HSPLIT
    start_row = tensor_index * TOK_DEV
    hit_table, weight_table, rank_table, position_table = route_tables(
        expert_ids, route_weights, experts, most_rows
    )
    hit_slot = pick_slot(hit_table, expert_count, slot_count, slot_index)
    weight_slot = pick_slot(weight_table, expert_count, slot_count, slot_index)
    position_slot = pick_slot(position_table, expert_count, slot_count, slot_index)
    slot_match = (hit_slot[:, :, None] == 1) & (
        position_slot[:, :, None] == jnp.arange(capacity, dtype=jnp.int32)[None, None, :]
    )
    head_sum = lax.psum(head_part.astype(jnp.bfloat16), "tensor").astype(jnp.float32)
    residual_full = lax.all_gather(residual, "tensor", axis=0, tiled=True)
    state_full = (residual_full.astype(jnp.float32) + head_sum).astype(jnp.bfloat16)
    hidden_state = lax.dynamic_slice_in_dim(state_full, start_row, TOK_DEV, 0)
    normed_full = norm_rows(state_full, norm_gain)
    source_rows = jnp.sum(
        jnp.where(slot_match, jnp.arange(step_rows, dtype=jnp.int32)[:, None, None], 0), axis=0
    )
    filled = jnp.any(slot_match, axis=0)
    outgoing = jnp.where(
        filled[:, :, None], jnp.take(normed_full, source_rows, axis=0), jnp.zeros((), jnp.bfloat16)
    )
    arrived_rows = lax.all_to_all(outgoing, "expert", split_axis=0, concat_axis=0, tiled=True)
    flat_rows = arrived_rows.reshape(-1, arrived_rows.shape[-1])
    gate_val = jnp.dot(flat_rows, w_gate[0], preferred_element_type=jnp.float32)
    up_val = jnp.dot(flat_rows, w_up[0], preferred_element_type=jnp.float32)
    inner = (jax.nn.silu(gate_val) * up_val).astype(jnp.bfloat16)
    result = jnp.dot(inner, w_down[0], preferred_element_type=jnp.float32).astype(jnp.bfloat16)
    computed = result.reshape(arrived_rows.shape)
    returned = lax.all_to_all(computed, "expert", split_axis=0, concat_axis=0, tiled=True)
    combine_weights = jnp.where(slot_match, weight_slot[:, :, None], 0.0).astype(jnp.bfloat16)
    expert_part = jnp.einsum(
        "njc,jcd->nd", combine_weights, returned, preferred_element_type=jnp.float32
    )
    expert_share = lax.psum_scatter(
        expert_part.astype(jnp.bfloat16), "tensor", scatter_dimension=0, tiled=True
    ).astype(jnp.float32)
    return (hidden_state.astype(jnp.float32) + expert_share).astype(jnp.bfloat16)


def weight_columns(expert_ids, route_weights, experts):
    named_mask = expert_ids[:, :, None] == jnp.arange(experts, dtype=jnp.int32)[None, None, :]
    return jnp.sum(
        jnp.where(named_mask, route_weights[:, :, None].astype(jnp.float32), 0.0), axis=1
    )


def attend(queries, keys_values, prefix_len):
    tensor_index = lax.axis_index("tensor")
    step_rows = queries.shape[0]
    per_device = queries.shape[1] // HD
    kv_index = tensor_index * per_device // (HEADS // KVH)
    cached = lax.dynamic_index_in_dim(keys_values[0], kv_index, 0, keepdims=False)
    key_rows = cached[:, :HD]
    value_rows = cached[:, HD:]
    context = cached.shape[0]
    query_rows = queries.reshape(step_rows, per_device, HD)
    scores = jnp.einsum(
        "nhd,cd->hnc", query_rows, key_rows, preferred_element_type=jnp.float32
    ) / math.sqrt(HD)
    columns = jnp.arange(context, dtype=jnp.int32)[None, :]
    positions = jnp.arange(step_rows, dtype=jnp.int32)[:, None]
    visible = ((columns < prefix_len[0]) | (columns >= PREFIX) & (columns - PREFIX <= positions))[
        None
    ]
    highest = jnp.max(jnp.where(visible, scores, -1e30), axis=-1, keepdims=True)
    weights = jnp.exp(jnp.where(visible, scores - highest, -1e30))
    summed = jnp.sum(weights, axis=-1)
    blended = jnp.einsum(
        "hnc,cd->nhd", weights.astype(jnp.bfloat16), value_rows, preferred_element_type=jnp.float32
    )
    return (
        (blended / jnp.transpose(summed)[:, :, None])
        .astype(jnp.bfloat16)
        .reshape(step_rows, per_device * HD)
    )


def dense_shards(
    queries,
    keys_values,
    prefix_len,
    out_proj,
    residual,
    norm_gain,
    expert_ids,
    route_weights,
    w_gate,
    w_up,
    w_down,
):
    tensor_count = lax.axis_size("tensor")
    expert_count = lax.axis_size("expert")
    slot_count = tensor_count // HSPLIT
    experts = expert_count * slot_count
    own_expert = lax.axis_index("expert") * slot_count + lax.axis_index("tensor") // HSPLIT
    weight_table = weight_columns(expert_ids, route_weights, experts).astype(jnp.bfloat16)
    weight_all = lax.all_gather(weight_table, "expert", axis=0, tiled=True)
    own_weight = lax.dynamic_slice_in_dim(weight_all, own_expert, 1, 1).astype(jnp.float32)
    attended = attend(queries, keys_values, prefix_len)
    attended_all = lax.all_gather(attended, "expert", axis=0, tiled=True)
    head_part = jnp.dot(attended_all, out_proj, preferred_element_type=jnp.float32)
    head_part = head_part.astype(jnp.bfloat16).reshape(
        expert_count, tensor_count, TOK_DEV, out_proj.shape[1]
    )
    head_sum = lax.psum_scatter(head_part, "tensor", scatter_dimension=1, tiled=True)
    head_sum = lax.all_to_all(
        head_sum.reshape(expert_count, TOK_DEV, -1), "expert", split_axis=0, concat_axis=2, tiled=True
    )[0]
    hidden_state = (residual.astype(jnp.float32) + head_sum.astype(jnp.float32)).astype(
        jnp.bfloat16
    )
    normed = norm_rows(hidden_state, norm_gain)
    normed_all = lax.all_gather(normed, ("expert", "tensor"), axis=0, tiled=True)
    gate_val = jnp.dot(normed_all, w_gate[0], preferred_element_type=jnp.float32)
    up_val = jnp.dot(normed_all, w_up[0], preferred_element_type=jnp.float32)
    inner = (jax.nn.silu(gate_val) * up_val).astype(jnp.bfloat16)
    result = jnp.dot(inner, w_down[0], preferred_element_type=jnp.float32)
    part = (result * own_weight).astype(jnp.bfloat16)
    expert_share = lax.psum_scatter(part, ("expert", "tensor"), scatter_dimension=0, tiled=True)
    return (hidden_state.astype(jnp.float32) + expert_share.astype(jnp.float32)).astype(
        jnp.bfloat16
    )


def solution(mesh):
    experts = mesh.shape["expert"] * mesh.shape["tensor"] // HSPLIT
    dense = experts == TOPK
    return jax.shard_map(
        dense_shards if dense else shards,
        mesh=mesh,
        in_specs=(
            P("expert", "tensor"),
            P("expert", None, None, None),
            P("expert"),
            P("tensor", "expert"),
            P(("expert", "tensor"), None),
            P(),
            P("expert", None),
            P("expert", None),
            P(("expert", "tensor"), None, None),
            P(("expert", "tensor"), None, None),
            P(("expert", "tensor"), None, None),
        ),
        out_specs=P(("expert", "tensor"), None),
        check_vma=False,
    )
```

```python
import math

import jax
import jax.numpy as jnp
from jax import lax
from jax.experimental import pallas as pl
from jax.experimental.pallas import tpu as pltpu
from jax.sharding import PartitionSpec as P

HEADS = 64
KVH = 4
HD = 128
TOPK = 8
HSPLIT = 4
TOK_DEV = 16
PREFIX = 1024


def norm_rows(hidden_state, norm_gain):
    values = hidden_state.astype(jnp.float32)
    factor = lax.rsqrt(jnp.mean(values * values, axis=-1, keepdims=True) + 1e-06)
    return (values * factor * norm_gain[None, :]).astype(jnp.bfloat16)


def route_tables(expert_ids, route_weights, experts, most_rows):
    total_rows = expert_ids.shape[0]
    named_mask = expert_ids[:, :, None] == jnp.arange(experts, dtype=jnp.int32)[None, None, :]
    hit_table = jnp.sum(named_mask.astype(jnp.int32), axis=1)
    weight_table = jnp.sum(
        jnp.where(named_mask, route_weights[:, :, None].astype(jnp.float32), 0.0), axis=1
    )
    grouped = hit_table.reshape(total_rows // TOK_DEV, TOK_DEV, experts)
    rank_table = (jnp.cumsum(grouped, axis=1) - grouped).reshape(total_rows, experts)
    share_index = (jnp.arange(total_rows, dtype=jnp.int32) // TOK_DEV)[:, None]
    position_table = share_index * most_rows + rank_table
    return (hit_table, weight_table, rank_table, position_table)


def pick_slot(table, expert_count, slot_count, slot_index):
    shaped = table.reshape(table.shape[0], expert_count, slot_count)
    return lax.dynamic_index_in_dim(shaped, slot_index, 2, keepdims=False)


def shards(
    queries,
    keys_values,
    prefix_len,
    out_proj,
    residual,
    norm_gain,
    expert_ids,
    route_weights,
    w_gate,
    w_up,
    w_down,
):
    tensor_count = lax.axis_size("tensor")
    expert_count = lax.axis_size("expert")
    tensor_index = lax.axis_index("tensor")
    step_rows = queries.shape[0]
    per_device = queries.shape[1] // HD
    group_size = HEADS // KVH
    kv_index = tensor_index * per_device // group_size
    cached = lax.dynamic_index_in_dim(keys_values[0], kv_index, 0, keepdims=False)
    key_rows = cached[:, :HD]
    value_rows = cached[:, HD:]
    context = cached.shape[0]
    query_rows = queries.reshape(step_rows, per_device, HD)
    scores = jnp.einsum(
        "nhd,cd->hnc", query_rows, key_rows, preferred_element_type=jnp.float32
    ) / math.sqrt(HD)
    columns = jnp.arange(context, dtype=jnp.int32)[None, :]
    positions = jnp.arange(step_rows, dtype=jnp.int32)[:, None]
    visible = ((columns < prefix_len[0]) | (columns >= PREFIX) & (columns - PREFIX <= positions))[
        None
    ]
    highest = jnp.max(jnp.where(visible, scores, -1e30), axis=-1, keepdims=True)
    weights = jnp.exp(jnp.where(visible, scores - highest, -1e30))
    summed = jnp.sum(weights, axis=-1)
    blended = jnp.einsum(
        "hnc,cd->nhd", weights.astype(jnp.bfloat16), value_rows, preferred_element_type=jnp.float32
    )
    attended = (
        (blended / jnp.transpose(summed)[:, :, None])
        .astype(jnp.bfloat16)
        .reshape(step_rows, per_device * HD)
    )
    head_part = jnp.dot(
        attended,
        lax.all_gather(out_proj, "expert", axis=1, tiled=True),
        preferred_element_type=jnp.float32,
    )
    slot_count = tensor_count // HSPLIT
    experts = expert_count * slot_count
    most_rows = min(TOK_DEV, max(2, TOK_DEV * TOPK // experts + 1))
    capacity = tensor_count * most_rows
    slot_index = tensor_index // HSPLIT
    start_row = tensor_index * TOK_DEV
    hit_table, weight_table, rank_table, position_table = route_tables(
        expert_ids, route_weights, experts, most_rows
    )
    hit_slot = pick_slot(hit_table, expert_count, slot_count, slot_index)
    weight_slot = pick_slot(weight_table, expert_count, slot_count, slot_index)
    position_slot = pick_slot(position_table, expert_count, slot_count, slot_index)
    slot_match = (hit_slot[:, :, None] == 1) & (
        position_slot[:, :, None] == jnp.arange(capacity, dtype=jnp.int32)[None, None, :]
    )
    head_sum = lax.psum(head_part.astype(jnp.bfloat16), "tensor").astype(jnp.float32)
    residual_full = lax.all_gather(residual, "tensor", axis=0, tiled=True)
    state_full = (residual_full.astype(jnp.float32) + head_sum).astype(jnp.bfloat16)
    hidden_state = lax.dynamic_slice_in_dim(state_full, start_row, TOK_DEV, 0)
    normed_full = norm_rows(state_full, norm_gain)
    source_rows = jnp.sum(
        jnp.where(slot_match, jnp.arange(step_rows, dtype=jnp.int32)[:, None, None], 0), axis=0
    )
    filled = jnp.any(slot_match, axis=0)
    outgoing = jnp.where(
        filled[:, :, None], jnp.take(normed_full, source_rows, axis=0), jnp.zeros((), jnp.bfloat16)
    )
    arrived_rows = lax.all_to_all(outgoing, "expert", split_axis=0, concat_axis=0, tiled=True)
    flat_rows = arrived_rows.reshape(-1, arrived_rows.shape[-1])
    gate_val = jnp.dot(flat_rows, w_gate[0], preferred_element_type=jnp.float32)
    up_val = jnp.dot(flat_rows, w_up[0], preferred_element_type=jnp.float32)
    inner = (jax.nn.silu(gate_val) * up_val).astype(jnp.bfloat16)
    result = jnp.dot(inner, w_down[0], preferred_element_type=jnp.float32).astype(jnp.bfloat16)
    computed = result.reshape(arrived_rows.shape)
    returned = lax.all_to_all(computed, "expert", split_axis=0, concat_axis=0, tiled=True)
    combine_weights = jnp.where(slot_match, weight_slot[:, :, None], 0.0).astype(jnp.bfloat16)
    expert_part = jnp.einsum(
        "njc,jcd->nd", combine_weights, returned, preferred_element_type=jnp.float32
    )
    expert_share = lax.psum_scatter(
        expert_part.astype(jnp.bfloat16), "tensor", scatter_dimension=0, tiled=True
    ).astype(jnp.float32)
    return (hidden_state.astype(jnp.float32) + expert_share).astype(jnp.bfloat16)


def weight_columns(expert_ids, route_weights, experts):
    named_mask = expert_ids[:, :, None] == jnp.arange(experts, dtype=jnp.int32)[None, None, :]
    return jnp.sum(
        jnp.where(named_mask, route_weights[:, :, None].astype(jnp.float32), 0.0), axis=1
    )


def attend(queries, keys_values, prefix_len):
    tensor_index = lax.axis_index("tensor")
    step_rows = queries.shape[0]
    per_device = queries.shape[1] // HD
    kv_index = tensor_index * per_device // (HEADS // KVH)
    cached = lax.dynamic_index_in_dim(keys_values[0], kv_index, 0, keepdims=False)
    key_rows = cached[:, :HD]
    value_rows = cached[:, HD:]
    context = cached.shape[0]
    query_rows = queries.reshape(step_rows, per_device, HD)
    scores = jnp.einsum(
        "nhd,cd->hnc", query_rows, key_rows, preferred_element_type=jnp.float32
    ) / math.sqrt(HD)
    columns = jnp.arange(context, dtype=jnp.int32)[None, :]
    positions = jnp.arange(step_rows, dtype=jnp.int32)[:, None]
    visible = ((columns < prefix_len[0]) | (columns >= PREFIX) & (columns - PREFIX <= positions))[
        None
    ]
    highest = jnp.max(jnp.where(visible, scores, -1e30), axis=-1, keepdims=True)
    weights = jnp.exp(jnp.where(visible, scores - highest, -1e30))
    summed = jnp.sum(weights, axis=-1)
    blended = jnp.einsum(
        "hnc,cd->nhd", weights.astype(jnp.bfloat16), value_rows, preferred_element_type=jnp.float32
    )
    return (
        (blended / jnp.transpose(summed)[:, :, None])
        .astype(jnp.bfloat16)
        .reshape(step_rows, per_device * HD)
    )


LANES = 128
COPIES = 128


def layer_kernel(
    attended,
    proj_hbm,
    residual,
    gain,
    route,
    gate_hbm,
    up_hbm,
    down_hbm,
    out,
    proj,
    gate,
    up,
    down,
    seen,
    heads,
    heads_sib,
    head_sum,
    heads_z,
    col_out,
    col_in,
    hidden,
    rows,
    part,
    part_sib,
    diag_y,
    diag_x,
    part_x,
    part_y,
    z_out,
    z_in,
    send_sem,
    recv_sem,
    load_sem,
):
    width = residual.shape[1]
    half = width // 2
    e = lax.axis_index("expert")
    t = lax.axis_index("tensor")
    x, y, z, c = e % 2, e // 2, t // 2, t % 2
    flat = [
        e,
        y * 2 + (1 - x),
        (1 - y) * 2 + x,
        (1 - y) * 2 + (1 - x),
    ]
    line = [(z + k) % 4 for k in range(4)]
    to_x, to_y, to_diag = (flat[1], t), (flat[2], t), (flat[3], t)
    to_sib = (e, z * 2 + (1 - c))
    to_z = [None] + [(e, line[k] * 2 + c) for k in range(1, 4)]

    loads = []
    for index, (source, target) in enumerate(
        ((proj_hbm, proj), (gate_hbm, gate), (up_hbm, up), (down_hbm, down))
    ):
        loads.append(pltpu.make_async_copy(source, target, load_sem.at[index]))
        loads[-1].start()

    barrier = pltpu.get_barrier_semaphore()
    for partner in (to_x, to_y, to_diag, to_sib, *to_z[1:]):
        pl.semaphore_signal(
            barrier, inc=1, device_id=partner, device_id_type=pl.DeviceIdType.MESH
        )
    pl.semaphore_wait(barrier, 7)

    sent = []

    def send(source, target, partner):
        number = len(sent)
        copy = pltpu.make_async_remote_copy(
            src_ref=source,
            dst_ref=target,
            send_sem=send_sem.at[number],
            recv_sem=recv_sem.at[number],
            device_id=partner,
            device_id_type=pl.DeviceIdType.MESH,
        )
        copy.start()
        sent.append(copy)
        return copy

    row_half = attended.shape[0] // 2
    top, low = pl.ds(0, row_half), pl.ds(row_half, row_half)
    x_top = send(attended.at[top], seen.at[0, top], to_x)
    y_low = send(attended.at[low], seen.at[1, low], to_y)
    x_low = send(attended.at[low], seen.at[0, low], to_x)
    y_top = send(attended.at[top], seen.at[1, top], to_y)

    def project(source, r):
        @pl.loop(0, proj.shape[1] // 256)
        def _(tile):
            columns = pl.ds(pl.multiple_of(tile * 256, 256), 256)
            value = jnp.dot(source[...], proj[:, columns], preferred_element_type=jnp.float32)
            heads[r, :, :, :, columns] = value.astype(jnp.bfloat16).reshape(4, 2, TOK_DEV, 256)

        return send(heads.at[r, :, 1 - c], heads_sib.at[r], to_sib)

    def add_cores(r, copy):
        copy.wait_recv()

        @pl.loop(0, 4)
        def _(place):
            head_sum[r, place] = (
                heads[r, place, c].astype(jnp.float32)
                + heads_sib[r, place].astype(jnp.float32)
            ).astype(jnp.bfloat16)

        return [
            send(head_sum.at[r, line[k]], heads_z.at[r, (4 - k) % 4], to_z[k])
            for k in (2, 1, 3)
        ]

    loads[0].wait()
    sib = [project(attended, 0), None, None, None]
    x_top.wait_recv()
    d_top = send(seen.at[0, top], seen.at[2, top], to_y)
    y_low.wait_recv()
    d_low = send(seen.at[1, low], seen.at[2, low], to_x)
    along = [None] * 4
    x_low.wait_recv()
    sib[1] = project(seen.at[0], 1)
    along[0] = add_cores(0, sib[0])
    y_top.wait_recv()
    sib[2] = project(seen.at[1], 2)
    along[1] = add_cores(1, sib[1])
    d_top.wait_recv()
    d_low.wait_recv()
    sib[3] = project(seen.at[2], 3)
    along[2] = add_cores(2, sib[2])
    along[3] = add_cores(3, sib[3])

    columns_in = [None] * 4
    for r in (1, 2, 3, 0):
        for copy in along[r]:
            copy.wait_recv()
        total = head_sum[r, z].astype(jnp.float32)
        for k in range(1, 4):
            total = total + heads_z[r, k].astype(jnp.float32)
        if r:
            col_out[r] = total.astype(jnp.bfloat16)
            columns_in[r] = send(col_out.at[r], col_in.at[r], (flat[r], t))
        else:
            col_in[0] = total.astype(jnp.bfloat16)
    quarter = width // 4
    square = jnp.zeros((TOK_DEV, 1), jnp.float32)
    for r in range(4):
        if r:
            columns_in[r].wait_recv()
        columns = pl.ds(pl.multiple_of(flat[r] * quarter, quarter), quarter)
        state = residual[:, columns].astype(jnp.float32) + col_in[r].astype(jnp.float32)
        state = state.astype(jnp.bfloat16).astype(jnp.float32)
        hidden[:, columns] = state
        square = square + jnp.sum(state * state, axis=1, keepdims=True)
    factor = lax.rsqrt(square / width + 1e-06)
    own = pl.ds(0, TOK_DEV)
    rows[0, own, pl.ds(0, width)] = (hidden[...] * factor * gain[...]).astype(jnp.bfloat16)
    rows[0, own, pl.ds(width, LANES)] = route[...]

    full = rows.shape[2]
    first, last = pl.ds(0, half), pl.ds(half, full - half)

    def block(r, d):
        return pl.ds((d * 4 + r) * TOK_DEV, TOK_DEV)

    order = (0, 1, 3, 2)
    z_rows = [None] + [
        send(rows.at[0, own], rows.at[(4 - k) % 4, own], to_z[k]) for k in range(1, 4)
    ]
    x_rows, y_rows, d_first, d_last = {}, {}, {}, {}
    other = {k: [] for k in order}

    def spread(k):
        if k:
            z_rows[(4 - k) % 4].wait_recv()
        x_rows[k] = send(rows.at[k, own], rows.at[k, block(1, 0)], to_x)
        y_rows[k] = send(rows.at[k, own], rows.at[k, block(2, 0)], to_y)
        other[k].append(send(rows.at[k, own], rows.at[k, block(0, 1)], to_sib))

    def pass_on(k):
        x_rows[k].wait_recv()
        d_first[k] = send(
            rows.at[k, block(1, 0), first], rows.at[k, block(3, 0), first], to_y
        )
        other[k].append(send(rows.at[k, block(1, 0)], rows.at[k, block(1, 1)], to_sib))
        y_rows[k].wait_recv()
        d_last[k] = send(rows.at[k, block(2, 0), last], rows.at[k, block(3, 0), last], to_x)
        other[k].append(send(rows.at[k, block(2, 0)], rows.at[k, block(2, 1)], to_sib))

    def complete(k):
        d_first[k].wait_recv()
        d_last[k].wait_recv()
        other[k].append(send(rows.at[k, block(3, 0)], rows.at[k, block(3, 1)], to_sib))

    own_expert = e * 2 + t // HSPLIT
    part_copies = {}

    def experts(k):
        for copy in other[k]:
            copy.wait_recv()
        values = rows.at[k, :, pl.ds(0, width)]
        gate_val = jnp.dot(values[...], gate[...], preferred_element_type=jnp.float32)
        up_val = jnp.dot(values[...], up[...], preferred_element_type=jnp.float32)
        inner = (gate_val / (1.0 + jnp.exp(-gate_val)) * up_val).astype(jnp.bfloat16)
        named = lax.broadcasted_iota(jnp.int32, (8 * TOK_DEV, LANES), 1) == own_expert
        weight = jnp.sum(
            jnp.where(named, rows[k, :, pl.ds(width, LANES)].astype(jnp.float32), 0.0),
            axis=1,
            keepdims=True,
        )

        @pl.loop(0, width // 512)
        def _(tile):
            columns = pl.ds(pl.multiple_of(tile * 512, 512), 512)
            value = jnp.dot(inner, down[:, columns], preferred_element_type=jnp.float32)
            part[k, :, columns] = (value * weight).astype(jnp.bfloat16)

        part_copies[k] = send(
            part.at[k, pl.ds(4 * TOK_DEV, 4 * TOK_DEV)], part_sib.at[k], to_sib
        )

    front, back = pl.ds(0, half), pl.ds(half, half)
    diag_copies, plane_copies = {}, {}

    def add(k, r, columns, other_ref):
        place = (k, block(r, 0), columns)
        part[place] = (
            part[place].astype(jnp.float32) + other_ref.astype(jnp.float32)
        ).astype(jnp.bfloat16)

    def give_diag(k):
        part_copies[k].wait_recv()

        @pl.loop(0, 4)
        def _(r):
            place = pl.ds(pl.multiple_of(r * TOK_DEV, TOK_DEV), TOK_DEV)
            part[k, place, :] = (
                part[k, place, :].astype(jnp.float32)
                + part_sib[k, place, :].astype(jnp.float32)
            ).astype(jnp.bfloat16)

        diag_copies[k] = (
            send(part.at[k, block(3, 0), front], diag_y.at[k], to_y),
            send(part.at[k, block(3, 0), back], diag_x.at[k], to_x),
        )
        plane_copies[k] = [
            send(part.at[k, block(1, 0), back], part_x.at[k, :, back], to_x),
            send(part.at[k, block(2, 0), front], part_y.at[k, :, front], to_y),
        ]

    def give_plane(k):
        from_y, from_x = diag_copies[k]
        from_y.wait_recv()
        add(k, 1, front, diag_y[k])
        plane_copies[k].append(
            send(part.at[k, block(1, 0), front], part_x.at[k, :, front], to_x)
        )
        from_x.wait_recv()
        add(k, 2, back, diag_x[k])
        plane_copies[k].append(
            send(part.at[k, block(2, 0), back], part_y.at[k, :, back], to_y)
        )

    z_copies = {}

    def give_line(k):
        for copy in plane_copies[k]:
            copy.wait_recv()
        total = (
            part[k, own, :].astype(jnp.float32)
            + part_x[k].astype(jnp.float32)
            + part_y[k].astype(jnp.float32)
        )
        if k:
            z_out[k] = total.astype(jnp.bfloat16)
            z_copies[k] = send(z_out.at[k], z_in.at[(4 - k) % 4], to_z[k])
        else:
            hidden[...] = hidden[...] + total

    a, b, f, g = order
    spread(a)
    spread(b)
    pass_on(a)
    for load in loads[1:]:
        load.wait()
    complete(a)
    spread(f)
    pass_on(b)
    experts(a)
    complete(b)
    spread(g)
    pass_on(f)
    give_diag(a)
    experts(b)
    complete(f)
    pass_on(g)
    give_plane(a)
    give_diag(b)
    experts(f)
    complete(g)
    give_line(a)
    give_plane(b)
    give_diag(f)
    experts(g)
    give_line(b)
    give_plane(f)
    give_diag(g)
    give_line(f)
    give_plane(g)
    give_line(g)
    total = hidden[...]
    for k in order[1:]:
        z_copies[k].wait_recv()
        total = total + z_in[(4 - k) % 4].astype(jnp.float32)
    out[...] = total.astype(jnp.bfloat16)
    for copy in sent:
        copy.wait_send()


def dense_shards(
    queries,
    keys_values,
    prefix_len,
    out_proj,
    residual,
    norm_gain,
    expert_ids,
    route_weights,
    w_gate,
    w_up,
    w_down,
):
    experts = lax.axis_size("expert") * lax.axis_size("tensor") // HSPLIT
    weight_table = weight_columns(expert_ids, route_weights, experts).astype(jnp.bfloat16)
    route = lax.dynamic_slice_in_dim(
        weight_table, lax.axis_index("tensor") * TOK_DEV, TOK_DEV, 0
    )
    route = jnp.pad(route, ((0, 0), (0, LANES - experts)))
    attended = attend(queries, keys_values, prefix_len)
    width = residual.shape[1]
    depth, cols = out_proj.shape
    seq = attended.shape[0]
    hid = w_gate.shape[2]
    bf = jnp.bfloat16
    vmem = pl.BlockSpec(memory_space=pltpu.VMEM)
    hbm = pl.BlockSpec(memory_space=pl.ANY)
    return pl.pallas_call(
        layer_kernel,
        out_shape=jax.ShapeDtypeStruct((TOK_DEV, width), bf),
        in_specs=[vmem, hbm, vmem, vmem, vmem, hbm, hbm, hbm],
        out_specs=vmem,
        scratch_shapes=[
            pltpu.VMEM((depth, cols), bf),
            pltpu.VMEM((width, hid), bf),
            pltpu.VMEM((width, hid), bf),
            pltpu.VMEM((hid, width), bf),
            pltpu.VMEM((3, seq, depth), bf),
            pltpu.VMEM((4, 4, 2, TOK_DEV, cols), bf),
            pltpu.VMEM((4, 4, TOK_DEV, cols), bf),
            pltpu.VMEM((4, 4, TOK_DEV, cols), bf),
            pltpu.VMEM((4, 4, TOK_DEV, cols), bf),
            pltpu.VMEM((4, TOK_DEV, cols), bf),
            pltpu.VMEM((4, TOK_DEV, cols), bf),
            pltpu.VMEM((TOK_DEV, width), jnp.float32),
            pltpu.VMEM((4, seq, width + LANES), bf),
            pltpu.VMEM((4, seq, width), bf),
            pltpu.VMEM((4, seq // 2, width), bf),
            pltpu.VMEM((4, TOK_DEV, width // 2), bf),
            pltpu.VMEM((4, TOK_DEV, width // 2), bf),
            pltpu.VMEM((4, TOK_DEV, width), bf),
            pltpu.VMEM((4, TOK_DEV, width), bf),
            pltpu.VMEM((4, TOK_DEV, width), bf),
            pltpu.VMEM((4, TOK_DEV, width), bf),
            pltpu.SemaphoreType.DMA((COPIES,)),
            pltpu.SemaphoreType.DMA((COPIES,)),
            pltpu.SemaphoreType.DMA((4,)),
        ],
        compiler_params=pltpu.CompilerParams(
            collective_id=0, has_side_effects=True, vmem_limit_bytes=48 * 1024 * 1024
        ),
    )(
        attended,
        out_proj,
        residual,
        norm_gain[None, :],
        route,
        w_gate[0],
        w_up[0],
        w_down[0],
    )


def solution(mesh):
    experts = mesh.shape["expert"] * mesh.shape["tensor"] // HSPLIT
    dense = experts == TOPK and mesh.shape["expert"] == 4 and mesh.shape["tensor"] == 8
    return jax.shard_map(
        dense_shards if dense else shards,
        mesh=mesh,
        in_specs=(
            P("expert", "tensor"),
            P("expert", None, None, None),
            P("expert"),
            P("tensor", "expert"),
            P(("expert", "tensor"), None),
            P(),
            P("expert", None),
            P("expert", None),
            P(("expert", "tensor"), None, None),
            P(("expert", "tensor"), None, None),
            P(("expert", "tensor"), None, None),
        ),
        out_specs=P(("expert", "tensor"), None),
        check_vma=False,
    )
```

```python
import math

import jax
import jax.numpy as jnp
from jax import lax
from jax.experimental import pallas as pl
from jax.experimental.pallas import tpu as pltpu
from jax.sharding import PartitionSpec as P

HEADS = 64
KVH = 4
HD = 128
TOPK = 8
HSPLIT = 4
TOK_DEV = 16
PREFIX = 1024


def norm_rows(hidden_state, norm_gain):
    values = hidden_state.astype(jnp.float32)
    factor = lax.rsqrt(jnp.mean(values * values, axis=-1, keepdims=True) + 1e-06)
    return (values * factor * norm_gain[None, :]).astype(jnp.bfloat16)


def route_tables(expert_ids, route_weights, experts, most_rows):
    total_rows = expert_ids.shape[0]
    named_mask = expert_ids[:, :, None] == jnp.arange(experts, dtype=jnp.int32)[None, None, :]
    hit_table = jnp.sum(named_mask.astype(jnp.int32), axis=1)
    weight_table = jnp.sum(
        jnp.where(named_mask, route_weights[:, :, None].astype(jnp.float32), 0.0), axis=1
    )
    grouped = hit_table.reshape(total_rows // TOK_DEV, TOK_DEV, experts)
    rank_table = (jnp.cumsum(grouped, axis=1) - grouped).reshape(total_rows, experts)
    share_index = (jnp.arange(total_rows, dtype=jnp.int32) // TOK_DEV)[:, None]
    position_table = share_index * most_rows + rank_table
    return (hit_table, weight_table, rank_table, position_table)


def pick_slot(table, expert_count, slot_count, slot_index):
    shaped = table.reshape(table.shape[0], expert_count, slot_count)
    return lax.dynamic_index_in_dim(shaped, slot_index, 2, keepdims=False)


def shards(
    queries,
    keys_values,
    prefix_len,
    out_proj,
    residual,
    norm_gain,
    expert_ids,
    route_weights,
    w_gate,
    w_up,
    w_down,
):
    tensor_count = lax.axis_size("tensor")
    expert_count = lax.axis_size("expert")
    tensor_index = lax.axis_index("tensor")
    step_rows = queries.shape[0]
    per_device = queries.shape[1] // HD
    group_size = HEADS // KVH
    kv_index = tensor_index * per_device // group_size
    cached = lax.dynamic_index_in_dim(keys_values[0], kv_index, 0, keepdims=False)
    key_rows = cached[:, :HD]
    value_rows = cached[:, HD:]
    context = cached.shape[0]
    query_rows = queries.reshape(step_rows, per_device, HD)
    scores = jnp.einsum(
        "nhd,cd->hnc", query_rows, key_rows, preferred_element_type=jnp.float32
    ) / math.sqrt(HD)
    columns = jnp.arange(context, dtype=jnp.int32)[None, :]
    positions = jnp.arange(step_rows, dtype=jnp.int32)[:, None]
    visible = ((columns < prefix_len[0]) | (columns >= PREFIX) & (columns - PREFIX <= positions))[
        None
    ]
    highest = jnp.max(jnp.where(visible, scores, -1e30), axis=-1, keepdims=True)
    weights = jnp.exp(jnp.where(visible, scores - highest, -1e30))
    summed = jnp.sum(weights, axis=-1)
    blended = jnp.einsum(
        "hnc,cd->nhd", weights.astype(jnp.bfloat16), value_rows, preferred_element_type=jnp.float32
    )
    attended = (
        (blended / jnp.transpose(summed)[:, :, None])
        .astype(jnp.bfloat16)
        .reshape(step_rows, per_device * HD)
    )
    head_part = jnp.dot(
        attended,
        lax.all_gather(out_proj, "expert", axis=1, tiled=True),
        preferred_element_type=jnp.float32,
    )
    slot_count = tensor_count // HSPLIT
    experts = expert_count * slot_count
    most_rows = min(TOK_DEV, max(2, TOK_DEV * TOPK // experts + 1))
    capacity = tensor_count * most_rows
    slot_index = tensor_index // HSPLIT
    start_row = tensor_index * TOK_DEV
    hit_table, weight_table, rank_table, position_table = route_tables(
        expert_ids, route_weights, experts, most_rows
    )
    hit_slot = pick_slot(hit_table, expert_count, slot_count, slot_index)
    weight_slot = pick_slot(weight_table, expert_count, slot_count, slot_index)
    position_slot = pick_slot(position_table, expert_count, slot_count, slot_index)
    slot_match = (hit_slot[:, :, None] == 1) & (
        position_slot[:, :, None] == jnp.arange(capacity, dtype=jnp.int32)[None, None, :]
    )
    head_sum = lax.psum(head_part.astype(jnp.bfloat16), "tensor").astype(jnp.float32)
    residual_full = lax.all_gather(residual, "tensor", axis=0, tiled=True)
    state_full = (residual_full.astype(jnp.float32) + head_sum).astype(jnp.bfloat16)
    hidden_state = lax.dynamic_slice_in_dim(state_full, start_row, TOK_DEV, 0)
    normed_full = norm_rows(state_full, norm_gain)
    source_rows = jnp.sum(
        jnp.where(slot_match, jnp.arange(step_rows, dtype=jnp.int32)[:, None, None], 0), axis=0
    )
    filled = jnp.any(slot_match, axis=0)
    outgoing = jnp.where(
        filled[:, :, None], jnp.take(normed_full, source_rows, axis=0), jnp.zeros((), jnp.bfloat16)
    )
    arrived_rows = lax.all_to_all(outgoing, "expert", split_axis=0, concat_axis=0, tiled=True)
    flat_rows = arrived_rows.reshape(-1, arrived_rows.shape[-1])
    gate_val = jnp.dot(flat_rows, w_gate[0], preferred_element_type=jnp.float32)
    up_val = jnp.dot(flat_rows, w_up[0], preferred_element_type=jnp.float32)
    inner = (jax.nn.silu(gate_val) * up_val).astype(jnp.bfloat16)
    result = jnp.dot(inner, w_down[0], preferred_element_type=jnp.float32).astype(jnp.bfloat16)
    computed = result.reshape(arrived_rows.shape)
    returned = lax.all_to_all(computed, "expert", split_axis=0, concat_axis=0, tiled=True)
    combine_weights = jnp.where(slot_match, weight_slot[:, :, None], 0.0).astype(jnp.bfloat16)
    expert_part = jnp.einsum(
        "njc,jcd->nd", combine_weights, returned, preferred_element_type=jnp.float32
    )
    expert_share = lax.psum_scatter(
        expert_part.astype(jnp.bfloat16), "tensor", scatter_dimension=0, tiled=True
    ).astype(jnp.float32)
    return (hidden_state.astype(jnp.float32) + expert_share).astype(jnp.bfloat16)


LANES = 128
COPIES = 128


def layer_kernel(
    queries_hbm,
    cache_hbm,
    prefix_len,
    proj_hbm,
    residual,
    gain,
    expert_ids,
    route_weights,
    gate_hbm,
    up_hbm,
    down_hbm,
    out,
    query,
    cached,
    bias,
    attended,
    proj,
    gate_up,
    down,
    seen,
    heads,
    heads_sib,
    head_sum,
    heads_z,
    col_out,
    col_in,
    hidden,
    rows,
    part,
    part_sib,
    diag_y,
    diag_x,
    part_x,
    part_y,
    z_out,
    z_in,
    send_sem,
    recv_sem,
    load_sem,
):
    width = residual.shape[1]
    half = width // 2
    e = lax.axis_index("expert")
    t = lax.axis_index("tensor")
    x, y, z, c = e % 2, e // 2, t // 2, t % 2
    flat = [
        e,
        y * 2 + (1 - x),
        (1 - y) * 2 + x,
        (1 - y) * 2 + (1 - x),
    ]
    line = [(z + k) % 4 for k in range(4)]
    to_x, to_y, to_diag = (flat[1], t), (flat[2], t), (flat[3], t)
    to_sib = (e, z * 2 + (1 - c))
    to_z = [None] + [(e, line[k] * 2 + c) for k in range(1, 4)]

    per_device = query.shape[1] // HD
    hid = gate_hbm.shape[1]
    kv_index = t * per_device // (HEADS // KVH)
    loads = []
    for index, (source, target) in enumerate(
        (
            (cache_hbm.at[kv_index], cached),
            (queries_hbm, query),
            (proj_hbm, proj),
            (gate_hbm, gate_up.at[:, pl.ds(0, hid)]),
            (up_hbm, gate_up.at[:, pl.ds(hid, hid)]),
            (down_hbm, down),
        )
    ):
        loads.append(pltpu.make_async_copy(source, target, load_sem.at[index]))
        loads[-1].start()

    barrier = pltpu.get_barrier_semaphore()
    for partner in (to_x, to_y, to_diag, to_sib, *to_z[1:]):
        pl.semaphore_signal(
            barrier, inc=1, device_id=partner, device_id_type=pl.DeviceIdType.MESH
        )
    sent = []

    def send(source, target, partner):
        number = len(sent)
        copy = pltpu.make_async_remote_copy(
            src_ref=source,
            dst_ref=target,
            send_sem=send_sem.at[number],
            recv_sem=recv_sem.at[number],
            device_id=partner,
            device_id_type=pl.DeviceIdType.MESH,
        )
        copy.start()
        sent.append(copy)
        return copy

    step_rows, context = bias.shape
    columns = lax.broadcasted_iota(jnp.int32, (step_rows, context), 1)
    positions = lax.broadcasted_iota(jnp.int32, (step_rows, context), 0)
    visible = (columns < prefix_len[0]) | (columns >= PREFIX) & (columns - PREFIX <= positions)
    bias[...] = jnp.where(visible, 0.0, -1e30)

    def attend_pair(pair):
        one, two = pl.ds(2 * pair * HD, HD), pl.ds((2 * pair + 1) * HD, HD)
        stacked = jnp.concatenate([query[:, one], query[:, two]], axis=0)
        scores = lax.dot_general(
            stacked,
            cached[:, pl.ds(0, HD)],
            (((1,), (1,)), ((), ())),
            preferred_element_type=jnp.float32,
        ).reshape(2, step_rows, context)
        scores = scores + bias[...][None]
        highest = jnp.max(scores, axis=-1, keepdims=True)
        weights = jnp.exp((scores - highest) * (1.0 / math.sqrt(HD)))
        summed = jnp.sum(weights, axis=-1, keepdims=True)
        blended = jnp.dot(
            weights.astype(jnp.bfloat16).reshape(2 * step_rows, context),
            cached[:, pl.ds(HD, HD)],
            preferred_element_type=jnp.float32,
        ).reshape(2, step_rows, HD)
        blended = (blended / summed).astype(jnp.bfloat16)
        attended[:, one] = blended[0]
        attended[:, two] = blended[1]

    depth_half = attended.shape[1] // 2
    top, low = pl.ds(0, depth_half), pl.ds(depth_half, depth_half)
    loads[0].wait()
    loads[1].wait()
    for pair in range(per_device // 4):
        attend_pair(pair)
    pl.semaphore_wait(barrier, 7)
    x_top = send(attended.at[:, top], seen.at[0, :, top], to_x)
    y_top = send(attended.at[:, top], seen.at[1, :, top], to_y)
    for pair in range(per_device // 4, per_device // 2):
        attend_pair(pair)
    y_low = send(attended.at[:, low], seen.at[1, :, low], to_y)
    x_low = send(attended.at[:, low], seen.at[0, :, low], to_x)

    def project(source, r):
        @pl.loop(0, proj.shape[1] // 256)
        def _(tile):
            columns = pl.ds(pl.multiple_of(tile * 256, 256), 256)
            value = jnp.dot(source[...], proj[:, columns], preferred_element_type=jnp.float32)
            heads[r, :, :, :, columns] = value.astype(jnp.bfloat16).reshape(4, 2, TOK_DEV, 256)

        return send(heads.at[r, :, 1 - c], heads_sib.at[r], to_sib)

    def add_cores(r, copy):
        copy.wait_recv()

        @pl.loop(0, 4)
        def _(place):
            head_sum[r, place] = (
                heads[r, place, c].astype(jnp.float32)
                + heads_sib[r, place].astype(jnp.float32)
            ).astype(jnp.bfloat16)

        return [
            send(head_sum.at[r, line[k]], heads_z.at[r, (4 - k) % 4], to_z[k])
            for k in (2, 1, 3)
        ]

    x_top.wait_recv()
    d_top = send(seen.at[0, :, top], seen.at[2, :, top], to_y)
    loads[2].wait()
    sib = [project(attended, 0), None, None, None]
    along = [None] * 4
    y_top.wait_recv()
    y_low.wait_recv()
    d_low = send(seen.at[1, :, low], seen.at[2, :, low], to_x)
    x_low.wait_recv()
    sib[1] = project(seen.at[0], 1)
    along[0] = add_cores(0, sib[0])
    sib[2] = project(seen.at[1], 2)
    along[1] = add_cores(1, sib[1])
    d_top.wait_recv()
    d_low.wait_recv()
    sib[3] = project(seen.at[2], 3)
    along[2] = add_cores(2, sib[2])
    along[3] = add_cores(3, sib[3])

    columns_in = [None] * 4
    for r in (1, 2, 3, 0):
        for copy in along[r]:
            copy.wait_recv()
        total = head_sum[r, z].astype(jnp.float32)
        for k in range(1, 4):
            total = total + heads_z[r, k].astype(jnp.float32)
        if r:
            col_out[r] = total.astype(jnp.bfloat16)
            columns_in[r] = send(col_out.at[r], col_in.at[r], (flat[r], t))
        else:
            col_in[0] = total.astype(jnp.bfloat16)
    quarter = width // 4
    square = jnp.zeros((TOK_DEV, 1), jnp.float32)
    for r in range(4):
        if r:
            columns_in[r].wait_recv()
        columns = pl.ds(pl.multiple_of(flat[r] * quarter, quarter), quarter)
        state = residual[:, columns].astype(jnp.float32) + col_in[r].astype(jnp.float32)
        state = state.astype(jnp.bfloat16).astype(jnp.float32)
        hidden[:, columns] = state
        square = square + jnp.sum(state * state, axis=1, keepdims=True)
    factor = lax.rsqrt(square / width + 1e-06)
    own = pl.ds(0, TOK_DEV)
    rows[0, own, pl.ds(0, width)] = (hidden[...] * factor * gain[...]).astype(jnp.bfloat16)
    lane = lax.broadcasted_iota(jnp.int32, (TOK_DEV, LANES), 1)
    mine = pl.ds(pl.multiple_of(t * TOK_DEV, TOK_DEV), TOK_DEV)
    ids, gains = expert_ids[mine, :], route_weights[mine, :].astype(jnp.float32)
    route = jnp.zeros((TOK_DEV, LANES), jnp.float32)
    for place in range(TOPK):
        route = route + jnp.where(
            ids[:, place : place + 1] == lane, gains[:, place : place + 1], 0.0
        )
    rows[0, own, pl.ds(width, LANES)] = route.astype(jnp.bfloat16)

    full = rows.shape[2]
    first, last = pl.ds(0, half), pl.ds(half, full - half)

    def block(r, d):
        return pl.ds((d * 4 + r) * TOK_DEV, TOK_DEV)

    order = (0, 1, 3, 2)
    z_rows = [None] + [
        send(rows.at[0, own], rows.at[(4 - k) % 4, own], to_z[k]) for k in range(1, 4)
    ]
    x_rows, y_rows, d_first, d_last = {}, {}, {}, {}
    other = {k: [] for k in order}

    def spread(k):
        if k:
            z_rows[(4 - k) % 4].wait_recv()
        x_rows[k] = send(rows.at[k, own], rows.at[k, block(1, 0)], to_x)
        y_rows[k] = send(rows.at[k, own], rows.at[k, block(2, 0)], to_y)
        other[k].append(send(rows.at[k, own], rows.at[k, block(0, 1)], to_sib))

    def pass_on(k):
        x_rows[k].wait_recv()
        d_first[k] = send(
            rows.at[k, block(1, 0), first], rows.at[k, block(3, 0), first], to_y
        )
        other[k].append(send(rows.at[k, block(1, 0)], rows.at[k, block(1, 1)], to_sib))
        y_rows[k].wait_recv()
        d_last[k] = send(rows.at[k, block(2, 0), last], rows.at[k, block(3, 0), last], to_x)
        other[k].append(send(rows.at[k, block(2, 0)], rows.at[k, block(2, 1)], to_sib))

    def complete(k):
        d_first[k].wait_recv()
        d_last[k].wait_recv()
        other[k].append(send(rows.at[k, block(3, 0)], rows.at[k, block(3, 1)], to_sib))

    own_expert = e * 2 + t // HSPLIT
    part_copies = {}

    def experts(k):
        for copy in other[k]:
            copy.wait_recv()
        values = rows.at[k, :, pl.ds(0, width)]
        both = jnp.dot(values[...], gate_up[...], preferred_element_type=jnp.float32)
        gate_val, up_val = both[:, :hid], both[:, hid:]
        inner = (gate_val / (1.0 + jnp.exp(-gate_val)) * up_val).astype(jnp.bfloat16)
        named = lax.broadcasted_iota(jnp.int32, (8 * TOK_DEV, LANES), 1) == own_expert
        weight = jnp.sum(
            jnp.where(named, rows[k, :, pl.ds(width, LANES)].astype(jnp.float32), 0.0),
            axis=1,
            keepdims=True,
        )

        @pl.loop(0, width // 512)
        def _(tile):
            columns = pl.ds(pl.multiple_of(tile * 512, 512), 512)
            value = jnp.dot(inner, down[:, columns], preferred_element_type=jnp.float32)
            part[k, :, columns] = (value * weight).astype(jnp.bfloat16)

        part_copies[k] = send(
            part.at[k, pl.ds(4 * TOK_DEV, 4 * TOK_DEV)], part_sib.at[k], to_sib
        )

    front, back = pl.ds(0, half), pl.ds(half, half)
    diag_copies, plane_copies = {}, {}

    def add(k, r, columns, other_ref):
        place = (k, block(r, 0), columns)
        part[place] = (
            part[place].astype(jnp.float32) + other_ref.astype(jnp.float32)
        ).astype(jnp.bfloat16)

    def give_diag(k):
        part_copies[k].wait_recv()

        @pl.loop(0, 4)
        def _(r):
            place = pl.ds(pl.multiple_of(r * TOK_DEV, TOK_DEV), TOK_DEV)
            part[k, place, :] = (
                part[k, place, :].astype(jnp.float32)
                + part_sib[k, place, :].astype(jnp.float32)
            ).astype(jnp.bfloat16)

        diag_copies[k] = (
            send(part.at[k, block(3, 0), front], diag_y.at[k], to_y),
            send(part.at[k, block(3, 0), back], diag_x.at[k], to_x),
        )
        plane_copies[k] = [
            send(part.at[k, block(1, 0), back], part_x.at[k, :, back], to_x),
            send(part.at[k, block(2, 0), front], part_y.at[k, :, front], to_y),
        ]

    def give_plane(k):
        from_y, from_x = diag_copies[k]
        from_y.wait_recv()
        add(k, 1, front, diag_y[k])
        plane_copies[k].append(
            send(part.at[k, block(1, 0), front], part_x.at[k, :, front], to_x)
        )
        from_x.wait_recv()
        add(k, 2, back, diag_x[k])
        plane_copies[k].append(
            send(part.at[k, block(2, 0), back], part_y.at[k, :, back], to_y)
        )

    z_copies = {}

    def give_line(k):
        for copy in plane_copies[k]:
            copy.wait_recv()
        total = (
            part[k, own, :].astype(jnp.float32)
            + part_x[k].astype(jnp.float32)
            + part_y[k].astype(jnp.float32)
        )
        if k:
            z_out[k] = total.astype(jnp.bfloat16)
            z_copies[k] = send(z_out.at[k], z_in.at[(4 - k) % 4], to_z[k])
        else:
            hidden[...] = hidden[...] + total

    a, b, f, g = order
    spread(a)
    spread(b)
    pass_on(a)
    for load in loads[3:]:
        load.wait()
    complete(a)
    spread(f)
    pass_on(b)
    experts(a)
    complete(b)
    spread(g)
    pass_on(f)
    give_diag(a)
    experts(b)
    complete(f)
    pass_on(g)
    give_plane(a)
    give_diag(b)
    experts(f)
    complete(g)
    give_line(a)
    give_plane(b)
    give_diag(f)
    experts(g)
    give_line(b)
    give_plane(f)
    give_diag(g)
    give_line(f)
    give_plane(g)
    give_line(g)
    total = hidden[...]
    for k in order[1:]:
        z_copies[k].wait_recv()
        total = total + z_in[(4 - k) % 4].astype(jnp.float32)
    out[...] = total.astype(jnp.bfloat16)
    for copy in sent:
        copy.wait_send()


def dense_shards(
    queries,
    keys_values,
    prefix_len,
    out_proj,
    residual,
    norm_gain,
    expert_ids,
    route_weights,
    w_gate,
    w_up,
    w_down,
):
    width = residual.shape[1]
    depth, cols = out_proj.shape
    seq = queries.shape[0]
    context = keys_values.shape[2]
    hid = w_gate.shape[2]
    bf = jnp.bfloat16
    vmem = pl.BlockSpec(memory_space=pltpu.VMEM)
    smem = pl.BlockSpec(memory_space=pltpu.SMEM)
    hbm = pl.BlockSpec(memory_space=pltpu.HBM)
    return pl.pallas_call(
        layer_kernel,
        out_shape=jax.ShapeDtypeStruct((TOK_DEV, width), bf),
        in_specs=[hbm, hbm, smem, hbm, vmem, vmem, vmem, vmem, hbm, hbm, hbm],
        out_specs=vmem,
        scratch_shapes=[
            pltpu.VMEM((seq, depth), bf),
            pltpu.VMEM((context, 2 * HD), bf),
            pltpu.VMEM((seq, context), jnp.float32),
            pltpu.VMEM((seq, depth), bf),
            pltpu.VMEM((depth, cols), bf),
            pltpu.VMEM((width, 2 * hid), bf),
            pltpu.VMEM((hid, width), bf),
            pltpu.VMEM((3, seq, depth), bf),
            pltpu.VMEM((4, 4, 2, TOK_DEV, cols), bf),
            pltpu.VMEM((4, 4, TOK_DEV, cols), bf),
            pltpu.VMEM((4, 4, TOK_DEV, cols), bf),
            pltpu.VMEM((4, 4, TOK_DEV, cols), bf),
            pltpu.VMEM((4, TOK_DEV, cols), bf),
            pltpu.VMEM((4, TOK_DEV, cols), bf),
            pltpu.VMEM((TOK_DEV, width), jnp.float32),
            pltpu.VMEM((4, seq, width + LANES), bf),
            pltpu.VMEM((4, seq, width), bf),
            pltpu.VMEM((4, seq // 2, width), bf),
            pltpu.VMEM((4, TOK_DEV, width // 2), bf),
            pltpu.VMEM((4, TOK_DEV, width // 2), bf),
            pltpu.VMEM((4, TOK_DEV, width), bf),
            pltpu.VMEM((4, TOK_DEV, width), bf),
            pltpu.VMEM((4, TOK_DEV, width), bf),
            pltpu.VMEM((4, TOK_DEV, width), bf),
            pltpu.SemaphoreType.DMA((COPIES,)),
            pltpu.SemaphoreType.DMA((COPIES,)),
            pltpu.SemaphoreType.DMA((6,)),
        ],
        compiler_params=pltpu.CompilerParams(
            collective_id=0, has_side_effects=True, vmem_limit_bytes=48 * 1024 * 1024
        ),
    )(
        queries,
        keys_values[0],
        prefix_len,
        out_proj,
        residual,
        norm_gain[None, :],
        expert_ids,
        route_weights,
        w_gate[0],
        w_up[0],
        w_down[0],
    )


def solution(mesh):
    experts = mesh.shape["expert"] * mesh.shape["tensor"] // HSPLIT
    dense = experts == TOPK and mesh.shape["expert"] == 4 and mesh.shape["tensor"] == 8
    return jax.shard_map(
        dense_shards if dense else shards,
        mesh=mesh,
        in_specs=(
            P("expert", "tensor"),
            P("expert", None, None, None),
            P("expert"),
            P("tensor", "expert"),
            P(("expert", "tensor"), None),
            P(),
            P("expert", None),
            P("expert", None),
            P(("expert", "tensor"), None, None),
            P(("expert", "tensor"), None, None),
            P(("expert", "tensor"), None, None),
        ),
        out_specs=P(("expert", "tensor"), None),
        check_vma=False,
    )
```

```python
import math

import jax
import jax.numpy as jnp
from jax import lax
from jax.experimental import pallas as pl
from jax.experimental.pallas import tpu as pltpu
from jax.sharding import PartitionSpec as P

HEADS = 64
KVH = 4
HD = 128
TOPK = 8
HSPLIT = 4
TOK_DEV = 16
PREFIX = 1024


def norm_rows(hidden_state, norm_gain):
    values = hidden_state.astype(jnp.float32)
    factor = lax.rsqrt(jnp.mean(values * values, axis=-1, keepdims=True) + 1e-06)
    return (values * factor * norm_gain[None, :]).astype(jnp.bfloat16)


def route_tables(expert_ids, route_weights, experts, most_rows):
    total_rows = expert_ids.shape[0]
    named_mask = expert_ids[:, :, None] == jnp.arange(experts, dtype=jnp.int32)[None, None, :]
    hit_table = jnp.sum(named_mask.astype(jnp.int32), axis=1)
    weight_table = jnp.sum(
        jnp.where(named_mask, route_weights[:, :, None].astype(jnp.float32), 0.0), axis=1
    )
    grouped = hit_table.reshape(total_rows // TOK_DEV, TOK_DEV, experts)
    rank_table = (jnp.cumsum(grouped, axis=1) - grouped).reshape(total_rows, experts)
    share_index = (jnp.arange(total_rows, dtype=jnp.int32) // TOK_DEV)[:, None]
    position_table = share_index * most_rows + rank_table
    return (hit_table, weight_table, rank_table, position_table)


def pick_slot(table, expert_count, slot_count, slot_index):
    shaped = table.reshape(table.shape[0], expert_count, slot_count)
    return lax.dynamic_index_in_dim(shaped, slot_index, 2, keepdims=False)


def shards(
    queries,
    keys_values,
    prefix_len,
    out_proj,
    residual,
    norm_gain,
    expert_ids,
    route_weights,
    w_gate,
    w_up,
    w_down,
):
    tensor_count = lax.axis_size("tensor")
    expert_count = lax.axis_size("expert")
    tensor_index = lax.axis_index("tensor")
    step_rows = queries.shape[0]
    per_device = queries.shape[1] // HD
    group_size = HEADS // KVH
    kv_index = tensor_index * per_device // group_size
    cached = lax.dynamic_index_in_dim(keys_values[0], kv_index, 0, keepdims=False)
    key_rows = cached[:, :HD]
    value_rows = cached[:, HD:]
    context = cached.shape[0]
    query_rows = queries.reshape(step_rows, per_device, HD)
    scores = jnp.einsum(
        "nhd,cd->hnc", query_rows, key_rows, preferred_element_type=jnp.float32
    ) / math.sqrt(HD)
    columns = jnp.arange(context, dtype=jnp.int32)[None, :]
    positions = jnp.arange(step_rows, dtype=jnp.int32)[:, None]
    visible = ((columns < prefix_len[0]) | (columns >= PREFIX) & (columns - PREFIX <= positions))[
        None
    ]
    highest = jnp.max(jnp.where(visible, scores, -1e30), axis=-1, keepdims=True)
    weights = jnp.exp(jnp.where(visible, scores - highest, -1e30))
    summed = jnp.sum(weights, axis=-1)
    blended = jnp.einsum(
        "hnc,cd->nhd", weights.astype(jnp.bfloat16), value_rows, preferred_element_type=jnp.float32
    )
    attended = (
        (blended / jnp.transpose(summed)[:, :, None])
        .astype(jnp.bfloat16)
        .reshape(step_rows, per_device * HD)
    )
    head_part = jnp.dot(
        attended,
        lax.all_gather(out_proj, "expert", axis=1, tiled=True),
        preferred_element_type=jnp.float32,
    )
    slot_count = tensor_count // HSPLIT
    experts = expert_count * slot_count
    most_rows = min(TOK_DEV, max(2, TOK_DEV * TOPK // experts + 1))
    capacity = tensor_count * most_rows
    slot_index = tensor_index // HSPLIT
    start_row = tensor_index * TOK_DEV
    hit_table, weight_table, rank_table, position_table = route_tables(
        expert_ids, route_weights, experts, most_rows
    )
    hit_slot = pick_slot(hit_table, expert_count, slot_count, slot_index)
    weight_slot = pick_slot(weight_table, expert_count, slot_count, slot_index)
    position_slot = pick_slot(position_table, expert_count, slot_count, slot_index)
    slot_match = (hit_slot[:, :, None] == 1) & (
        position_slot[:, :, None] == jnp.arange(capacity, dtype=jnp.int32)[None, None, :]
    )
    head_sum = lax.psum(head_part.astype(jnp.bfloat16), "tensor").astype(jnp.float32)
    residual_full = lax.all_gather(residual, "tensor", axis=0, tiled=True)
    state_full = (residual_full.astype(jnp.float32) + head_sum).astype(jnp.bfloat16)
    hidden_state = lax.dynamic_slice_in_dim(state_full, start_row, TOK_DEV, 0)
    normed_full = norm_rows(state_full, norm_gain)
    source_rows = jnp.sum(
        jnp.where(slot_match, jnp.arange(step_rows, dtype=jnp.int32)[:, None, None], 0), axis=0
    )
    filled = jnp.any(slot_match, axis=0)
    outgoing = jnp.where(
        filled[:, :, None], jnp.take(normed_full, source_rows, axis=0), jnp.zeros((), jnp.bfloat16)
    )
    arrived_rows = lax.all_to_all(outgoing, "expert", split_axis=0, concat_axis=0, tiled=True)
    flat_rows = arrived_rows.reshape(-1, arrived_rows.shape[-1])
    gate_val = jnp.dot(flat_rows, w_gate[0], preferred_element_type=jnp.float32)
    up_val = jnp.dot(flat_rows, w_up[0], preferred_element_type=jnp.float32)
    inner = (jax.nn.silu(gate_val) * up_val).astype(jnp.bfloat16)
    result = jnp.dot(inner, w_down[0], preferred_element_type=jnp.float32).astype(jnp.bfloat16)
    computed = result.reshape(arrived_rows.shape)
    returned = lax.all_to_all(computed, "expert", split_axis=0, concat_axis=0, tiled=True)
    combine_weights = jnp.where(slot_match, weight_slot[:, :, None], 0.0).astype(jnp.bfloat16)
    expert_part = jnp.einsum(
        "njc,jcd->nd", combine_weights, returned, preferred_element_type=jnp.float32
    )
    expert_share = lax.psum_scatter(
        expert_part.astype(jnp.bfloat16), "tensor", scatter_dimension=0, tiled=True
    ).astype(jnp.float32)
    return (hidden_state.astype(jnp.float32) + expert_share).astype(jnp.bfloat16)


LANES = 128
EXTRA = 64
COPIES = 128


def layer_kernel(
    queries_hbm,
    cache_hbm,
    table,
    proj_hbm,
    residual_hbm,
    gain_hbm,
    gate_hbm,
    up_hbm,
    down_hbm,
    out,
    query,
    cached,
    bias,
    attended,
    proj,
    residual,
    gain,
    gate_up,
    down,
    tables,
    seen,
    heads,
    heads_sib,
    head_sum,
    heads_z,
    res_in,
    hidden,
    rows,
    part,
    part_sib,
    diag_y,
    diag_x,
    part_x,
    part_y,
    z_out,
    z_in,
    send_sem,
    recv_sem,
    load_sem,
):
    width = residual.shape[1]
    half = width // 2
    e = lax.axis_index("expert")
    t = lax.axis_index("tensor")
    x, y, z, c = e % 2, e // 2, t // 2, t % 2
    flat = [
        e,
        y * 2 + (1 - x),
        (1 - y) * 2 + x,
        (1 - y) * 2 + (1 - x),
    ]
    line = [(z + k) % 4 for k in range(4)]
    to_x, to_y, to_diag = (flat[1], t), (flat[2], t), (flat[3], t)
    to_sib = (e, z * 2 + (1 - c))
    to_z = [None] + [(e, line[k] * 2 + c) for k in range(1, 4)]

    per_device = query.shape[1] // HD
    hid = gate_hbm.shape[1]
    kv_index = t * per_device // (HEADS // KVH)
    loads = []
    for index, (source, target) in enumerate(
        (
            (cache_hbm.at[kv_index], cached),
            (queries_hbm, query),
            (residual_hbm, residual),
            (gain_hbm, gain),
            (proj_hbm, proj),
            (gate_hbm, gate_up.at[:, pl.ds(0, hid)]),
            (up_hbm, gate_up.at[:, pl.ds(hid, hid)]),
            (down_hbm, down),
        )
    ):
        loads.append(pltpu.make_async_copy(source, target, load_sem.at[index]))
        loads[-1].start()

    barrier = pltpu.get_barrier_semaphore()
    for partner in (to_x, to_y, to_diag, to_sib, *to_z[1:]):
        pl.semaphore_signal(
            barrier, inc=1, device_id=partner, device_id_type=pl.DeviceIdType.MESH
        )
    sent = []

    def send(source, target, partner):
        number = len(sent)
        copy = pltpu.make_async_remote_copy(
            src_ref=source,
            dst_ref=target,
            send_sem=send_sem.at[number],
            recv_sem=recv_sem.at[number],
            device_id=partner,
            device_id_type=pl.DeviceIdType.MESH,
        )
        copy.start()
        sent.append(copy)
        return copy

    step_rows, context = bias.shape
    columns = lax.broadcasted_iota(jnp.int32, (step_rows, context), 1)
    positions = lax.broadcasted_iota(jnp.int32, (step_rows, context), 0)
    live = table[0:1, EXTRA : EXTRA + 1].astype(jnp.int32)
    visible = (columns < live) | (columns >= PREFIX) & (columns - PREFIX <= positions)
    bias[...] = jnp.where(visible, 0.0, -1e30)

    def attend_pair(pair):
        one, two = pl.ds(2 * pair * HD, HD), pl.ds((2 * pair + 1) * HD, HD)
        stacked = jnp.concatenate([query[:, one], query[:, two]], axis=0)
        scores = lax.dot_general(
            stacked,
            cached[:, pl.ds(0, HD)],
            (((1,), (1,)), ((), ())),
            preferred_element_type=jnp.float32,
        ).reshape(2, step_rows, context)
        scores = scores + bias[...][None]
        highest = jnp.max(scores, axis=-1, keepdims=True)
        weights = jnp.exp((scores - highest) * (1.0 / math.sqrt(HD)))
        summed = jnp.sum(weights, axis=-1, keepdims=True)
        blended = jnp.dot(
            weights.astype(jnp.bfloat16).reshape(2 * step_rows, context),
            cached[:, pl.ds(HD, HD)],
            preferred_element_type=jnp.float32,
        ).reshape(2, step_rows, HD)
        blended = (blended / summed).astype(jnp.bfloat16)
        attended[:, one] = blended[0]
        attended[:, two] = blended[1]

    depth_half = attended.shape[1] // 2
    top, low = pl.ds(0, depth_half), pl.ds(depth_half, depth_half)
    loads[0].wait()
    loads[1].wait()
    for pair in range(per_device // 4):
        attend_pair(pair)
    pl.semaphore_wait(barrier, 7)
    x_top = send(attended.at[:, top], seen.at[0, :, top], to_x)
    y_top = send(attended.at[:, top], seen.at[1, :, top], to_y)
    quarter = width // 4

    def column_block(r):
        return pl.ds(pl.multiple_of(flat[r] * quarter, quarter), quarter)

    loads[2].wait()
    tables[e] = table[...].astype(jnp.bfloat16).reshape(tables.shape[1:])
    early = []
    for r in (1, 2, 3):
        early.append(send(residual.at[:, column_block(r)], res_in.at[r], (flat[r], t)))
        early.append(send(tables.at[e], tables.at[e], (flat[r], t)))
    for pair in range(per_device // 4, per_device // 2):
        attend_pair(pair)
    y_low = send(attended.at[:, low], seen.at[1, :, low], to_y)
    x_low = send(attended.at[:, low], seen.at[0, :, low], to_x)

    def project(source, r):
        @pl.loop(0, proj.shape[1] // 256)
        def _(tile):
            columns = pl.ds(pl.multiple_of(tile * 256, 256), 256)
            value = jnp.dot(source[...], proj[:, columns], preferred_element_type=jnp.float32)
            heads[r, :, :, :, columns] = value.astype(jnp.bfloat16).reshape(4, 2, TOK_DEV, 256)

        return send(heads.at[r, :, 1 - c], heads_sib.at[r], to_sib)

    def add_cores(r, copy):
        copy.wait_recv()

        @pl.loop(0, 4)
        def _(place):
            head_sum[r, place] = (
                heads[r, place, c].astype(jnp.float32)
                + heads_sib[r, place].astype(jnp.float32)
            ).astype(jnp.bfloat16)

        return [
            send(head_sum.at[r, line[k]], heads_z.at[r, (4 - k) % 4], to_z[k])
            for k in (2, 1, 3)
        ]

    x_top.wait_recv()
    d_top = send(seen.at[0, :, top], seen.at[2, :, top], to_y)
    loads[3].wait()
    loads[4].wait()
    sib = [project(attended, 0), None, None, None]
    along = [None] * 4
    y_top.wait_recv()
    y_low.wait_recv()
    d_low = send(seen.at[1, :, low], seen.at[2, :, low], to_x)
    x_low.wait_recv()
    sib[1] = project(seen.at[0], 1)
    along[0] = add_cores(0, sib[0])
    sib[2] = project(seen.at[1], 2)
    along[1] = add_cores(1, sib[1])
    d_top.wait_recv()
    d_low.wait_recv()
    sib[3] = project(seen.at[2], 3)
    along[2] = add_cores(2, sib[2])
    along[3] = add_cores(3, sib[3])

    pairs = (y, 1 - y)
    order = (0, 1, 3, 2)
    z_rows, x_rows, y_rows, d_first, d_last = {}, {}, {}, {}, {}
    other = {}

    def state(r, place):
        for copy in along[r]:
            copy.wait_recv()
        total = head_sum[r, z].astype(jnp.float32)
        for k in range(1, 4):
            total = total + heads_z[r, k].astype(jnp.float32)
        own = residual[:, column_block(0)] if r == 0 else res_in[r]
        rows[(0, 0, 0, *place)] = (total + own.astype(jnp.float32)).astype(jnp.bfloat16)

    def launch(h):
        piece = rows.at[0, 0, 0, pairs[h]]
        for k in (2, 1, 3):
            z_rows[k, h] = send(piece, rows.at[(4 - k) % 4, 0, 0, pairs[h]], to_z[k])
        x_rows[0, h] = send(piece, rows.at[0, 1, 0, pairs[h]], to_x)
        y_rows[0, h] = send(piece, rows.at[0, 2, 0, pairs[h]], to_y)

    def share(k, r):
        other[k, r] = send(rows.at[k, r, 0], rows.at[k, r, 1], to_sib)

    def spread(k):
        for h in (0, 1):
            z_rows[(4 - k) % 4, h].wait_recv()
            piece = rows.at[k, 0, 0, pairs[h]]
            x_rows[k, h] = send(piece, rows.at[k, 1, 0, pairs[h]], to_x)
            y_rows[k, h] = send(piece, rows.at[k, 2, 0, pairs[h]], to_y)
        share(k, 0)

    def pass_on(k):
        x_rows[k, 0].wait_recv()
        d_first[k] = send(rows.at[k, 1, 0, y], rows.at[k, 3, 0, y], to_y)
        y_rows[k, 0].wait_recv()
        y_rows[k, 1].wait_recv()
        d_last[k] = send(rows.at[k, 2, 0, y], rows.at[k, 3, 0, y], to_x)
        x_rows[k, 1].wait_recv()
        share(k, 1)
        share(k, 2)

    def complete(k):
        d_first[k].wait_recv()
        d_last[k].wait_recv()
        share(k, 3)

    for copy in early:
        copy.wait_recv()
    state(0, (y, x))
    state(1, (y, 1 - x))
    launch(0)
    state(2, (1 - y, x))
    state(3, (1 - y, 1 - x))
    launch(1)
    share(0, 0)

    own_expert = e * 2 + t // HSPLIT
    slab = 8 * TOK_DEV
    part_copies = {}

    def experts(k):
        square = jnp.zeros((slab, 1), jnp.float32)
        both = jnp.zeros((slab, 2 * hid), jnp.float32)
        for r in range(4):
            other[k, r].wait_recv()
            values = rows[k, r].reshape(slab, quarter).astype(jnp.float32)
            square = square + jnp.sum(values * values, axis=1, keepdims=True)
            scaled = (values * gain[:, column_block(r)]).astype(jnp.bfloat16)
            both = both + jnp.dot(
                scaled, gate_up[column_block(r), :], preferred_element_type=jnp.float32
            )
        both = both * lax.rsqrt(square / width + 1e-06)
        gate_val, up_val = both[:, :hid], both[:, hid:]
        inner = (gate_val / (1.0 + jnp.exp(-gate_val)) * up_val).astype(jnp.bfloat16)
        named = lax.broadcasted_iota(jnp.int32, (slab, LANES), 1) == own_expert
        listed = jnp.concatenate(
            [tables[s, line[k] * 2 + core] for core in (c, 1 - c) for s in range(4)], axis=0
        )
        weight = jnp.sum(jnp.where(named, listed.astype(jnp.float32), 0.0), axis=1, keepdims=True)

        @pl.loop(0, width // 512)
        def _(tile):
            columns = pl.ds(pl.multiple_of(tile * 512, 512), 512)
            value = jnp.dot(inner, down[:, columns], preferred_element_type=jnp.float32)
            part[k, :, :, :, columns] = (
                (value * weight).astype(jnp.bfloat16).reshape(2, 4, TOK_DEV, 512)
            )

        part_copies[k] = send(part.at[k, 1], part_sib.at[k], to_sib)

    half = width // 2
    front, back = pl.ds(0, half), pl.ds(half, half)
    diag_copies, plane_copies = {}, {}

    def add(k, r, columns, other_ref):
        place = (k, 0, flat[r], slice(None), columns)
        part[place] = (
            part[place].astype(jnp.float32) + other_ref.astype(jnp.float32)
        ).astype(jnp.bfloat16)

    def give_diag(k):
        part_copies[k].wait_recv()

        @pl.loop(0, 4)
        def _(s):
            part[k, 0, s] = (
                part[k, 0, s].astype(jnp.float32) + part_sib[k, s].astype(jnp.float32)
            ).astype(jnp.bfloat16)

        diag_copies[k] = (
            send(part.at[k, 0, flat[3], :, front], diag_y.at[k], to_y),
            send(part.at[k, 0, flat[3], :, back], diag_x.at[k], to_x),
        )
        plane_copies[k] = [
            send(part.at[k, 0, flat[1], :, back], part_x.at[k, :, back], to_x),
            send(part.at[k, 0, flat[2], :, front], part_y.at[k, :, front], to_y),
        ]

    def give_plane(k):
        from_y, from_x = diag_copies[k]
        from_y.wait_recv()
        add(k, 1, front, diag_y[k])
        plane_copies[k].append(
            send(part.at[k, 0, flat[1], :, front], part_x.at[k, :, front], to_x)
        )
        from_x.wait_recv()
        add(k, 2, back, diag_x[k])
        plane_copies[k].append(
            send(part.at[k, 0, flat[2], :, back], part_y.at[k, :, back], to_y)
        )

    z_copies = {}

    def give_line(k):
        for copy in plane_copies[k]:
            copy.wait_recv()
        total = (
            part[k, 0, e].astype(jnp.float32)
            + part_x[k].astype(jnp.float32)
            + part_y[k].astype(jnp.float32)
        )
        if k:
            z_out[k] = total.astype(jnp.bfloat16)
            z_copies[k] = send(z_out.at[k], z_in.at[(4 - k) % 4], to_z[k])
        else:
            hidden[...] = total

    a, b, f, g = order
    spread(b)
    pass_on(a)
    for load in loads[5:]:
        load.wait()
    complete(a)
    spread(f)
    pass_on(b)
    experts(a)
    complete(b)
    spread(g)
    pass_on(f)
    give_diag(a)
    experts(b)
    complete(f)
    pass_on(g)
    give_plane(a)
    give_diag(b)
    experts(f)
    complete(g)
    give_line(a)
    give_plane(b)
    give_diag(f)
    experts(g)
    give_line(b)
    give_plane(f)
    give_diag(g)
    give_line(f)
    give_plane(g)
    give_line(g)
    total = hidden[...]
    for k in order[1:]:
        z_copies[k].wait_recv()
        total = total + z_in[(4 - k) % 4].astype(jnp.float32)
    hidden[...] = total
    for r in range(4):
        columns = column_block(r)
        out[:, columns] = (
            hidden[:, columns] + rows[0, r, 0, y, x].astype(jnp.float32)
        ).astype(jnp.bfloat16)
    for copy in sent:
        copy.wait_send()


def dense_shards(
    queries,
    keys_values,
    prefix_len,
    out_proj,
    residual,
    norm_gain,
    expert_ids,
    route_weights,
    w_gate,
    w_up,
    w_down,
):
    lanes = jnp.arange(LANES, dtype=jnp.int32)
    named_mask = expert_ids[:, :, None] == lanes[None, None, :]
    table = jnp.sum(
        jnp.where(named_mask, route_weights[:, :, None].astype(jnp.float32), 0.0), axis=1
    )
    table = jnp.where(lanes[None, :] == EXTRA, prefix_len.astype(jnp.float32)[:, None], table)
    width = residual.shape[1]
    depth, cols = out_proj.shape
    seq = queries.shape[0]
    context = keys_values.shape[2]
    hid = w_gate.shape[2]
    bf = jnp.bfloat16
    vmem = pl.BlockSpec(memory_space=pltpu.VMEM)
    hbm = pl.BlockSpec(memory_space=pltpu.HBM)
    return pl.pallas_call(
        layer_kernel,
        out_shape=jax.ShapeDtypeStruct((TOK_DEV, width), bf),
        in_specs=[hbm, hbm, vmem, hbm, hbm, hbm, hbm, hbm, hbm],
        out_specs=vmem,
        scratch_shapes=[
            pltpu.VMEM((seq, depth), bf),
            pltpu.VMEM((context, 2 * HD), bf),
            pltpu.VMEM((seq, context), jnp.float32),
            pltpu.VMEM((seq, depth), bf),
            pltpu.VMEM((depth, cols), bf),
            pltpu.VMEM((TOK_DEV, width), bf),
            pltpu.VMEM((1, width), jnp.float32),
            pltpu.VMEM((width, 2 * hid), bf),
            pltpu.VMEM((hid, width), bf),
            pltpu.VMEM((4, 8, TOK_DEV, LANES), bf),
            pltpu.VMEM((3, seq, depth), bf),
            pltpu.VMEM((4, 4, 2, TOK_DEV, cols), bf),
            pltpu.VMEM((4, 4, TOK_DEV, cols), bf),
            pltpu.VMEM((4, 4, TOK_DEV, cols), bf),
            pltpu.VMEM((4, 4, TOK_DEV, cols), bf),
            pltpu.VMEM((4, TOK_DEV, cols), bf),
            pltpu.VMEM((TOK_DEV, width), jnp.float32),
            pltpu.VMEM((4, 4, 2, 2, 2, TOK_DEV, cols), bf),
            pltpu.VMEM((4, 2, 4, TOK_DEV, width), bf),
            pltpu.VMEM((4, 4, TOK_DEV, width), bf),
            pltpu.VMEM((4, TOK_DEV, width // 2), bf),
            pltpu.VMEM((4, TOK_DEV, width // 2), bf),
            pltpu.VMEM((4, TOK_DEV, width), bf),
            pltpu.VMEM((4, TOK_DEV, width), bf),
            pltpu.VMEM((4, TOK_DEV, width), bf),
            pltpu.VMEM((4, TOK_DEV, width), bf),
            pltpu.SemaphoreType.DMA((COPIES,)),
            pltpu.SemaphoreType.DMA((COPIES,)),
            pltpu.SemaphoreType.DMA((8,)),
        ],
        compiler_params=pltpu.CompilerParams(
            collective_id=0, has_side_effects=True, vmem_limit_bytes=48 * 1024 * 1024
        ),
    )(
        queries,
        keys_values[0],
        table,
        out_proj,
        residual,
        norm_gain[None, :],
        w_gate[0],
        w_up[0],
        w_down[0],
    )


def solution(mesh):
    experts = mesh.shape["expert"] * mesh.shape["tensor"] // HSPLIT
    dense = experts == TOPK and mesh.shape["expert"] == 4 and mesh.shape["tensor"] == 8
    return jax.shard_map(
        dense_shards if dense else shards,
        mesh=mesh,
        in_specs=(
            P("expert", "tensor"),
            P("expert", None, None, None),
            P("expert"),
            P("tensor", "expert"),
            P(("expert", "tensor"), None),
            P(),
            P("expert", None),
            P("expert", None),
            P(("expert", "tensor"), None, None),
            P(("expert", "tensor"), None, None),
            P(("expert", "tensor"), None, None),
        ),
        out_specs=P(("expert", "tensor"), None),
        check_vma=False,
    )
```

```python
import math

import jax
import jax.numpy as jnp
from jax import lax
from jax.experimental import pallas as pl
from jax.experimental.pallas import tpu as pltpu
from jax.sharding import PartitionSpec as P

HEADS = 64
KVH = 4
HD = 128
TOPK = 8
HSPLIT = 4
TOK_DEV = 16
PREFIX = 1024


def norm_rows(hidden_state, norm_gain):
    values = hidden_state.astype(jnp.float32)
    factor = lax.rsqrt(jnp.mean(values * values, axis=-1, keepdims=True) + 1e-06)
    return (values * factor * norm_gain[None, :]).astype(jnp.bfloat16)


def route_tables(expert_ids, route_weights, experts, most_rows):
    total_rows = expert_ids.shape[0]
    named_mask = expert_ids[:, :, None] == jnp.arange(experts, dtype=jnp.int32)[None, None, :]
    hit_table = jnp.sum(named_mask.astype(jnp.int32), axis=1)
    weight_table = jnp.sum(
        jnp.where(named_mask, route_weights[:, :, None].astype(jnp.float32), 0.0), axis=1
    )
    grouped = hit_table.reshape(total_rows // TOK_DEV, TOK_DEV, experts)
    rank_table = (jnp.cumsum(grouped, axis=1) - grouped).reshape(total_rows, experts)
    share_index = (jnp.arange(total_rows, dtype=jnp.int32) // TOK_DEV)[:, None]
    position_table = share_index * most_rows + rank_table
    return (hit_table, weight_table, rank_table, position_table)


def pick_slot(table, expert_count, slot_count, slot_index):
    shaped = table.reshape(table.shape[0], expert_count, slot_count)
    return lax.dynamic_index_in_dim(shaped, slot_index, 2, keepdims=False)


def shards(
    queries,
    keys_values,
    prefix_len,
    out_proj,
    residual,
    norm_gain,
    expert_ids,
    route_weights,
    w_gate,
    w_up,
    w_down,
):
    tensor_count = lax.axis_size("tensor")
    expert_count = lax.axis_size("expert")
    tensor_index = lax.axis_index("tensor")
    step_rows = queries.shape[0]
    per_device = queries.shape[1] // HD
    group_size = HEADS // KVH
    kv_index = tensor_index * per_device // group_size
    cached = lax.dynamic_index_in_dim(keys_values[0], kv_index, 0, keepdims=False)
    key_rows = cached[:, :HD]
    value_rows = cached[:, HD:]
    context = cached.shape[0]
    query_rows = queries.reshape(step_rows, per_device, HD)
    scores = jnp.einsum(
        "nhd,cd->hnc", query_rows, key_rows, preferred_element_type=jnp.float32
    ) / math.sqrt(HD)
    columns = jnp.arange(context, dtype=jnp.int32)[None, :]
    positions = jnp.arange(step_rows, dtype=jnp.int32)[:, None]
    visible = ((columns < prefix_len[0]) | (columns >= PREFIX) & (columns - PREFIX <= positions))[
        None
    ]
    highest = jnp.max(jnp.where(visible, scores, -1e30), axis=-1, keepdims=True)
    weights = jnp.exp(jnp.where(visible, scores - highest, -1e30))
    summed = jnp.sum(weights, axis=-1)
    blended = jnp.einsum(
        "hnc,cd->nhd", weights.astype(jnp.bfloat16), value_rows, preferred_element_type=jnp.float32
    )
    attended = (
        (blended / jnp.transpose(summed)[:, :, None])
        .astype(jnp.bfloat16)
        .reshape(step_rows, per_device * HD)
    )
    head_part = jnp.dot(
        attended,
        lax.all_gather(out_proj, "expert", axis=1, tiled=True),
        preferred_element_type=jnp.float32,
    )
    slot_count = tensor_count // HSPLIT
    experts = expert_count * slot_count
    most_rows = min(TOK_DEV, max(2, TOK_DEV * TOPK // experts + 1))
    capacity = tensor_count * most_rows
    slot_index = tensor_index // HSPLIT
    start_row = tensor_index * TOK_DEV
    hit_table, weight_table, rank_table, position_table = route_tables(
        expert_ids, route_weights, experts, most_rows
    )
    hit_slot = pick_slot(hit_table, expert_count, slot_count, slot_index)
    weight_slot = pick_slot(weight_table, expert_count, slot_count, slot_index)
    position_slot = pick_slot(position_table, expert_count, slot_count, slot_index)
    slot_match = (hit_slot[:, :, None] == 1) & (
        position_slot[:, :, None] == jnp.arange(capacity, dtype=jnp.int32)[None, None, :]
    )
    head_sum = lax.psum(head_part.astype(jnp.bfloat16), "tensor").astype(jnp.float32)
    residual_full = lax.all_gather(residual, "tensor", axis=0, tiled=True)
    state_full = (residual_full.astype(jnp.float32) + head_sum).astype(jnp.bfloat16)
    hidden_state = lax.dynamic_slice_in_dim(state_full, start_row, TOK_DEV, 0)
    normed_full = norm_rows(state_full, norm_gain)
    source_rows = jnp.sum(
        jnp.where(slot_match, jnp.arange(step_rows, dtype=jnp.int32)[:, None, None], 0), axis=0
    )
    filled = jnp.any(slot_match, axis=0)
    outgoing = jnp.where(
        filled[:, :, None], jnp.take(normed_full, source_rows, axis=0), jnp.zeros((), jnp.bfloat16)
    )
    arrived_rows = lax.all_to_all(outgoing, "expert", split_axis=0, concat_axis=0, tiled=True)
    flat_rows = arrived_rows.reshape(-1, arrived_rows.shape[-1])
    gate_val = jnp.dot(flat_rows, w_gate[0], preferred_element_type=jnp.float32)
    up_val = jnp.dot(flat_rows, w_up[0], preferred_element_type=jnp.float32)
    inner = (jax.nn.silu(gate_val) * up_val).astype(jnp.bfloat16)
    result = jnp.dot(inner, w_down[0], preferred_element_type=jnp.float32).astype(jnp.bfloat16)
    computed = result.reshape(arrived_rows.shape)
    returned = lax.all_to_all(computed, "expert", split_axis=0, concat_axis=0, tiled=True)
    combine_weights = jnp.where(slot_match, weight_slot[:, :, None], 0.0).astype(jnp.bfloat16)
    expert_part = jnp.einsum(
        "njc,jcd->nd", combine_weights, returned, preferred_element_type=jnp.float32
    )
    expert_share = lax.psum_scatter(
        expert_part.astype(jnp.bfloat16), "tensor", scatter_dimension=0, tiled=True
    ).astype(jnp.float32)
    return (hidden_state.astype(jnp.float32) + expert_share).astype(jnp.bfloat16)


LANES = 128
COPIES = 128


def layer_kernel(
    queries_hbm,
    cache_hbm,
    prefix_len,
    ids_hbm,
    gains_hbm,
    proj_hbm,
    residual_hbm,
    gain_hbm,
    gate_hbm,
    up_hbm,
    down_hbm,
    out,
    query,
    cached,
    bias,
    attended,
    proj,
    residual,
    gain,
    gate_up,
    down,
    ids,
    gains,
    tables,
    seen,
    heads,
    heads_sib,
    head_sum,
    heads_z,
    res_in,
    hidden,
    rows,
    part,
    part_sib,
    diag_y,
    diag_x,
    part_x,
    part_y,
    z_out,
    z_in,
    send_sem,
    recv_sem,
    load_sem,
):
    width = residual.shape[1]
    half = width // 2
    e = lax.axis_index("expert")
    t = lax.axis_index("tensor")
    x, y, z, c = e % 2, e // 2, t // 2, t % 2
    flat = [
        e,
        y * 2 + (1 - x),
        (1 - y) * 2 + x,
        (1 - y) * 2 + (1 - x),
    ]
    line = [(z + k) % 4 for k in range(4)]
    to_x, to_y, to_diag = (flat[1], t), (flat[2], t), (flat[3], t)
    to_sib = (e, z * 2 + (1 - c))
    to_z = [None] + [(e, line[k] * 2 + c) for k in range(1, 4)]

    per_device = query.shape[1] // HD
    hid = gate_hbm.shape[1]
    kv_index = t * per_device // (HEADS // KVH)
    loads = []
    for index, (source, target) in enumerate(
        (
            (cache_hbm.at[kv_index], cached),
            (queries_hbm, query),
            (residual_hbm, residual),
            (gain_hbm, gain),
            (proj_hbm, proj),
            (gate_hbm, gate_up.at[:, pl.ds(0, hid)]),
            (up_hbm, gate_up.at[:, pl.ds(hid, hid)]),
            (down_hbm, down),
            (ids_hbm, ids),
            (gains_hbm, gains),
        )
    ):
        loads.append(pltpu.make_async_copy(source, target, load_sem.at[index]))
    for index in (0, 1, 8, 9, 2, 3, 4, 5, 6, 7):
        loads[index].start()

    barrier = pltpu.get_barrier_semaphore()
    for partner in (to_x, to_y, to_diag, to_sib, *to_z[1:]):
        pl.semaphore_signal(
            barrier, inc=1, device_id=partner, device_id_type=pl.DeviceIdType.MESH
        )
    sent = []

    def send(source, target, partner):
        number = len(sent)
        copy = pltpu.make_async_remote_copy(
            src_ref=source,
            dst_ref=target,
            send_sem=send_sem.at[number],
            recv_sem=recv_sem.at[number],
            device_id=partner,
            device_id_type=pl.DeviceIdType.MESH,
        )
        copy.start()
        sent.append(copy)
        return copy

    step_rows, context = bias.shape
    columns = lax.broadcasted_iota(jnp.int32, (step_rows, context), 1)
    positions = lax.broadcasted_iota(jnp.int32, (step_rows, context), 0)
    visible = (columns < prefix_len[0]) | (columns >= PREFIX) & (columns - PREFIX <= positions)
    bias[...] = jnp.where(visible, 0.0, -1e30)

    def attend_pair(pair):
        one, two = pl.ds(2 * pair * HD, HD), pl.ds((2 * pair + 1) * HD, HD)
        stacked = jnp.concatenate([query[:, one], query[:, two]], axis=0)
        scores = lax.dot_general(
            stacked,
            cached[:, pl.ds(0, HD)],
            (((1,), (1,)), ((), ())),
            preferred_element_type=jnp.float32,
        ).reshape(2, step_rows, context)
        scores = scores + bias[...][None]
        highest = jnp.max(scores, axis=-1, keepdims=True)
        weights = jnp.exp((scores - highest) * (1.0 / math.sqrt(HD)))
        summed = jnp.sum(weights, axis=-1, keepdims=True)
        blended = jnp.dot(
            weights.astype(jnp.bfloat16).reshape(2 * step_rows, context),
            cached[:, pl.ds(HD, HD)],
            preferred_element_type=jnp.float32,
        ).reshape(2, step_rows, HD)
        blended = (blended / summed).astype(jnp.bfloat16)
        attended[:, one] = blended[0]
        attended[:, two] = blended[1]

    depth_half = attended.shape[1] // 2
    top, low = pl.ds(0, depth_half), pl.ds(depth_half, depth_half)
    loads[0].wait()
    loads[1].wait()
    for pair in range(per_device // 4):
        attend_pair(pair)
    pl.semaphore_wait(barrier, 7)
    x_top = send(attended.at[:, top], seen.at[0, :, top], to_x)
    y_top = send(attended.at[:, top], seen.at[1, :, top], to_y)
    quarter = width // 4

    def column_block(r):
        return pl.ds(pl.multiple_of(flat[r] * quarter, quarter), quarter)

    loads[2].wait()
    loads[8].wait()
    loads[9].wait()
    along_rows = lax.broadcasted_iota(jnp.int32, (LANES, step_rows), 0)
    along_lanes = lax.broadcasted_iota(jnp.int32, (LANES, step_rows), 1)
    turned = jnp.zeros((LANES, step_rows), jnp.float32)
    for place in range(TOPK):
        turned = turned + jnp.where(
            ids[place : place + 1, :] == along_rows, gains[place : place + 1, :], 0.0
        )
    unit = jnp.where(along_rows == along_lanes, 1.0, 0.0).astype(jnp.bfloat16)
    table = lax.dot_general(
        unit,
        turned.astype(jnp.bfloat16),
        (((1,), (1,)), ((), ())),
        preferred_element_type=jnp.float32,
    )
    tables[e] = table.astype(jnp.bfloat16).reshape(tables.shape[1:])
    early = []
    for r in (1, 2, 3):
        early.append(send(residual.at[:, column_block(r)], res_in.at[r], (flat[r], t)))
        early.append(send(tables.at[e], tables.at[e], (flat[r], t)))
    for pair in range(per_device // 4, per_device // 2):
        attend_pair(pair)
    y_low = send(attended.at[:, low], seen.at[1, :, low], to_y)
    x_low = send(attended.at[:, low], seen.at[0, :, low], to_x)

    def project(source, r):
        @pl.loop(0, proj.shape[1] // 256)
        def _(tile):
            columns = pl.ds(pl.multiple_of(tile * 256, 256), 256)
            value = jnp.dot(source[...], proj[:, columns], preferred_element_type=jnp.float32)
            heads[r, :, :, :, columns] = value.astype(jnp.bfloat16).reshape(4, 2, TOK_DEV, 256)

        return send(heads.at[r, :, 1 - c], heads_sib.at[r], to_sib)

    def add_cores(r, copy):
        copy.wait_recv()

        @pl.loop(0, 4)
        def _(place):
            head_sum[r, place] = (
                heads[r, place, c].astype(jnp.float32)
                + heads_sib[r, place].astype(jnp.float32)
            ).astype(jnp.bfloat16)

        return [
            send(head_sum.at[r, line[k]], heads_z.at[r, (4 - k) % 4], to_z[k])
            for k in (2, 1, 3)
        ]

    x_top.wait_recv()
    d_top = send(seen.at[0, :, top], seen.at[2, :, top], to_y)
    loads[3].wait()
    loads[4].wait()
    sib = [project(attended, 0), None, None, None]
    along = [None] * 4
    y_top.wait_recv()
    y_low.wait_recv()
    d_low = send(seen.at[1, :, low], seen.at[2, :, low], to_x)
    x_low.wait_recv()
    sib[1] = project(seen.at[0], 1)
    along[0] = add_cores(0, sib[0])
    sib[2] = project(seen.at[1], 2)
    along[1] = add_cores(1, sib[1])
    d_top.wait_recv()
    d_low.wait_recv()
    sib[3] = project(seen.at[2], 3)
    along[2] = add_cores(2, sib[2])
    along[3] = add_cores(3, sib[3])

    pairs = (y, 1 - y)
    order = (0, 1, 3, 2)
    z_rows, x_rows, y_rows, d_first, d_last = {}, {}, {}, {}, {}
    other = {}

    def state(r, place):
        for copy in along[r]:
            copy.wait_recv()
        total = head_sum[r, z].astype(jnp.float32)
        for k in range(1, 4):
            total = total + heads_z[r, k].astype(jnp.float32)
        own = residual[:, column_block(0)] if r == 0 else res_in[r]
        rows[(0, 0, 0, *place)] = (total + own.astype(jnp.float32)).astype(jnp.bfloat16)

    def launch(h):
        piece = rows.at[0, 0, 0, pairs[h]]
        for k in (2, 1, 3):
            z_rows[k, h] = send(piece, rows.at[(4 - k) % 4, 0, 0, pairs[h]], to_z[k])
        x_rows[0, h] = send(piece, rows.at[0, 1, 0, pairs[h]], to_x)
        y_rows[0, h] = send(piece, rows.at[0, 2, 0, pairs[h]], to_y)

    def share(k, r):
        other[k, r] = send(rows.at[k, r, 0], rows.at[k, r, 1], to_sib)

    def spread(k):
        for h in (0, 1):
            z_rows[(4 - k) % 4, h].wait_recv()
            piece = rows.at[k, 0, 0, pairs[h]]
            x_rows[k, h] = send(piece, rows.at[k, 1, 0, pairs[h]], to_x)
            y_rows[k, h] = send(piece, rows.at[k, 2, 0, pairs[h]], to_y)
        share(k, 0)

    def pass_on(k):
        x_rows[k, 0].wait_recv()
        d_first[k] = send(rows.at[k, 1, 0, y], rows.at[k, 3, 0, y], to_y)
        y_rows[k, 0].wait_recv()
        y_rows[k, 1].wait_recv()
        d_last[k] = send(rows.at[k, 2, 0, y], rows.at[k, 3, 0, y], to_x)
        x_rows[k, 1].wait_recv()
        share(k, 1)
        share(k, 2)

    def complete(k):
        d_first[k].wait_recv()
        d_last[k].wait_recv()
        share(k, 3)

    for copy in early:
        copy.wait_recv()
    state(0, (y, x))
    state(1, (y, 1 - x))
    launch(0)
    state(2, (1 - y, x))
    state(3, (1 - y, 1 - x))
    launch(1)
    share(0, 0)

    own_expert = e * 2 + t // HSPLIT
    slab = 8 * TOK_DEV
    part_copies = {}

    def experts(k):
        square = jnp.zeros((slab, 1), jnp.float32)
        both = jnp.zeros((slab, 2 * hid), jnp.float32)
        for r in range(4):
            other[k, r].wait_recv()
            values = rows[k, r].reshape(slab, quarter).astype(jnp.float32)
            square = square + jnp.sum(values * values, axis=1, keepdims=True)
            scaled = (values * gain[:, column_block(r)]).astype(jnp.bfloat16)
            both = both + jnp.dot(
                scaled, gate_up[column_block(r), :], preferred_element_type=jnp.float32
            )
        both = both * lax.rsqrt(square / width + 1e-06)
        gate_val, up_val = both[:, :hid], both[:, hid:]
        inner = (gate_val / (1.0 + jnp.exp(-gate_val)) * up_val).astype(jnp.bfloat16)
        named = lax.broadcasted_iota(jnp.int32, (slab, LANES), 1) == own_expert
        listed = jnp.concatenate(
            [tables[s, line[k] * 2 + core] for core in (c, 1 - c) for s in range(4)], axis=0
        )
        weight = jnp.sum(jnp.where(named, listed.astype(jnp.float32), 0.0), axis=1, keepdims=True)

        @pl.loop(0, width // 512)
        def _(tile):
            columns = pl.ds(pl.multiple_of(tile * 512, 512), 512)
            value = jnp.dot(inner, down[:, columns], preferred_element_type=jnp.float32)
            part[k, :, :, :, columns] = (
                (value * weight).astype(jnp.bfloat16).reshape(2, 4, TOK_DEV, 512)
            )

        part_copies[k] = send(part.at[k, 1], part_sib.at[k], to_sib)

    half = width // 2
    front, back = pl.ds(0, half), pl.ds(half, half)
    diag_copies, plane_copies = {}, {}

    def add(k, r, columns, other_ref):
        place = (k, 0, flat[r], slice(None), columns)
        part[place] = (
            part[place].astype(jnp.float32) + other_ref.astype(jnp.float32)
        ).astype(jnp.bfloat16)

    def give_diag(k):
        part_copies[k].wait_recv()

        @pl.loop(0, 4)
        def _(s):
            part[k, 0, s] = (
                part[k, 0, s].astype(jnp.float32) + part_sib[k, s].astype(jnp.float32)
            ).astype(jnp.bfloat16)

        diag_copies[k] = (
            send(part.at[k, 0, flat[3], :, front], diag_y.at[k], to_y),
            send(part.at[k, 0, flat[3], :, back], diag_x.at[k], to_x),
        )
        plane_copies[k] = [
            send(part.at[k, 0, flat[1], :, back], part_x.at[k, :, back], to_x),
            send(part.at[k, 0, flat[2], :, front], part_y.at[k, :, front], to_y),
        ]

    def give_plane(k):
        from_y, from_x = diag_copies[k]
        from_y.wait_recv()
        add(k, 1, front, diag_y[k])
        plane_copies[k].append(
            send(part.at[k, 0, flat[1], :, front], part_x.at[k, :, front], to_x)
        )
        from_x.wait_recv()
        add(k, 2, back, diag_x[k])
        plane_copies[k].append(
            send(part.at[k, 0, flat[2], :, back], part_y.at[k, :, back], to_y)
        )

    z_copies = {}

    def give_line(k):
        for copy in plane_copies[k]:
            copy.wait_recv()
        total = (
            part[k, 0, e].astype(jnp.float32)
            + part_x[k].astype(jnp.float32)
            + part_y[k].astype(jnp.float32)
        )
        if k:
            z_out[k] = total.astype(jnp.bfloat16)
            z_copies[k] = send(z_out.at[k], z_in.at[(4 - k) % 4], to_z[k])
        else:
            hidden[...] = total

    a, b, f, g = order
    spread(b)
    pass_on(a)
    complete(a)
    spread(f)
    pass_on(b)
    for load in loads[5:8]:
        load.wait()
    experts(a)
    complete(b)
    spread(g)
    pass_on(f)
    experts(b)
    complete(f)
    pass_on(g)
    give_diag(b)
    experts(f)
    complete(g)
    give_plane(b)
    give_diag(f)
    experts(g)
    give_line(b)
    give_plane(f)
    give_diag(g)
    give_diag(a)
    give_line(f)
    give_plane(g)
    give_plane(a)
    give_line(g)
    give_line(a)
    total = hidden[...]
    for k in order[1:]:
        z_copies[k].wait_recv()
        total = total + z_in[(4 - k) % 4].astype(jnp.float32)
    hidden[...] = total
    for r in range(4):
        columns = column_block(r)
        out[:, columns] = (
            hidden[:, columns] + rows[0, r, 0, y, x].astype(jnp.float32)
        ).astype(jnp.bfloat16)
    for copy in sent:
        copy.wait_send()


def dense_shards(
    queries,
    keys_values,
    prefix_len,
    out_proj,
    residual,
    norm_gain,
    expert_ids,
    route_weights,
    w_gate,
    w_up,
    w_down,
):
    width = residual.shape[1]
    depth, cols = out_proj.shape
    seq = queries.shape[0]
    context = keys_values.shape[2]
    hid = w_gate.shape[2]
    bf = jnp.bfloat16
    vmem = pl.BlockSpec(memory_space=pltpu.VMEM)
    smem = pl.BlockSpec(memory_space=pltpu.SMEM)
    hbm = pl.BlockSpec(memory_space=pltpu.HBM)
    return pl.pallas_call(
        layer_kernel,
        out_shape=jax.ShapeDtypeStruct((TOK_DEV, width), bf),
        in_specs=[hbm, hbm, smem, hbm, hbm, hbm, hbm, hbm, hbm, hbm, hbm],
        out_specs=vmem,
        scratch_shapes=[
            pltpu.VMEM((seq, depth), bf),
            pltpu.VMEM((context, 2 * HD), bf),
            pltpu.VMEM((seq, context), jnp.float32),
            pltpu.VMEM((seq, depth), bf),
            pltpu.VMEM((depth, cols), bf),
            pltpu.VMEM((TOK_DEV, width), bf),
            pltpu.VMEM((1, width), jnp.float32),
            pltpu.VMEM((width, 2 * hid), bf),
            pltpu.VMEM((hid, width), bf),
            pltpu.VMEM((TOPK, seq), jnp.int32),
            pltpu.VMEM((TOPK, seq), jnp.float32),
            pltpu.VMEM((4, 8, TOK_DEV, LANES), bf),
            pltpu.VMEM((3, seq, depth), bf),
            pltpu.VMEM((4, 4, 2, TOK_DEV, cols), bf),
            pltpu.VMEM((4, 4, TOK_DEV, cols), bf),
            pltpu.VMEM((4, 4, TOK_DEV, cols), bf),
            pltpu.VMEM((4, 4, TOK_DEV, cols), bf),
            pltpu.VMEM((4, TOK_DEV, cols), bf),
            pltpu.VMEM((TOK_DEV, width), jnp.float32),
            pltpu.VMEM((4, 4, 2, 2, 2, TOK_DEV, cols), bf),
            pltpu.VMEM((4, 2, 4, TOK_DEV, width), bf),
            pltpu.VMEM((4, 4, TOK_DEV, width), bf),
            pltpu.VMEM((4, TOK_DEV, width // 2), bf),
            pltpu.VMEM((4, TOK_DEV, width // 2), bf),
            pltpu.VMEM((4, TOK_DEV, width), bf),
            pltpu.VMEM((4, TOK_DEV, width), bf),
            pltpu.VMEM((4, TOK_DEV, width), bf),
            pltpu.VMEM((4, TOK_DEV, width), bf),
            pltpu.SemaphoreType.DMA((COPIES,)),
            pltpu.SemaphoreType.DMA((COPIES,)),
            pltpu.SemaphoreType.DMA((10,)),
        ],
        compiler_params=pltpu.CompilerParams(
            collective_id=0, has_side_effects=True, vmem_limit_bytes=63 * 1024 * 1024
        ),
    )(
        queries,
        keys_values[0],
        prefix_len,
        expert_ids.T,
        route_weights.T.astype(jnp.float32),
        out_proj,
        residual,
        norm_gain[None, :],
        w_gate[0],
        w_up[0],
        w_down[0],
    )


def solution(mesh):
    experts = mesh.shape["expert"] * mesh.shape["tensor"] // HSPLIT
    dense = experts == TOPK and mesh.shape["expert"] == 4 and mesh.shape["tensor"] == 8
    return jax.shard_map(
        dense_shards if dense else shards,
        mesh=mesh,
        in_specs=(
            P("expert", "tensor"),
            P("expert", None, None, None),
            P("expert"),
            P("tensor", "expert"),
            P(("expert", "tensor"), None),
            P(),
            P("expert", None),
            P("expert", None),
            P(("expert", "tensor"), None, None),
            P(("expert", "tensor"), None, None),
            P(("expert", "tensor"), None, None),
        ),
        out_specs=P(("expert", "tensor"), None),
        check_vma=False,
    )
```

```python
import math

import jax
import jax.numpy as jnp
from jax import lax
from jax.experimental import pallas as pl
from jax.experimental.pallas import tpu as pltpu
from jax.sharding import PartitionSpec as P

HEADS = 64
KVH = 4
HD = 128
TOPK = 8
HSPLIT = 4
TOK_DEV = 16
PREFIX = 1024


def norm_rows(hidden_state, norm_gain):
    values = hidden_state.astype(jnp.float32)
    factor = lax.rsqrt(jnp.mean(values * values, axis=-1, keepdims=True) + 1e-06)
    return (values * factor * norm_gain[None, :]).astype(jnp.bfloat16)


def route_tables(expert_ids, route_weights, experts, most_rows):
    total_rows = expert_ids.shape[0]
    named_mask = expert_ids[:, :, None] == jnp.arange(experts, dtype=jnp.int32)[None, None, :]
    hit_table = jnp.sum(named_mask.astype(jnp.int32), axis=1)
    weight_table = jnp.sum(
        jnp.where(named_mask, route_weights[:, :, None].astype(jnp.float32), 0.0), axis=1
    )
    grouped = hit_table.reshape(total_rows // TOK_DEV, TOK_DEV, experts)
    rank_table = (jnp.cumsum(grouped, axis=1) - grouped).reshape(total_rows, experts)
    share_index = (jnp.arange(total_rows, dtype=jnp.int32) // TOK_DEV)[:, None]
    position_table = share_index * most_rows + rank_table
    return (hit_table, weight_table, rank_table, position_table)


def pick_slot(table, expert_count, slot_count, slot_index):
    shaped = table.reshape(table.shape[0], expert_count, slot_count)
    return lax.dynamic_index_in_dim(shaped, slot_index, 2, keepdims=False)


def shards(
    queries,
    keys_values,
    prefix_len,
    out_proj,
    residual,
    norm_gain,
    expert_ids,
    route_weights,
    w_gate,
    w_up,
    w_down,
):
    tensor_count = lax.axis_size("tensor")
    expert_count = lax.axis_size("expert")
    tensor_index = lax.axis_index("tensor")
    step_rows = queries.shape[0]
    per_device = queries.shape[1] // HD
    group_size = HEADS // KVH
    kv_index = tensor_index * per_device // group_size
    cached = lax.dynamic_index_in_dim(keys_values[0], kv_index, 0, keepdims=False)
    key_rows = cached[:, :HD]
    value_rows = cached[:, HD:]
    context = cached.shape[0]
    query_rows = queries.reshape(step_rows, per_device, HD)
    scores = jnp.einsum(
        "nhd,cd->hnc", query_rows, key_rows, preferred_element_type=jnp.float32
    ) / math.sqrt(HD)
    columns = jnp.arange(context, dtype=jnp.int32)[None, :]
    positions = jnp.arange(step_rows, dtype=jnp.int32)[:, None]
    visible = ((columns < prefix_len[0]) | (columns >= PREFIX) & (columns - PREFIX <= positions))[
        None
    ]
    highest = jnp.max(jnp.where(visible, scores, -1e30), axis=-1, keepdims=True)
    weights = jnp.exp(jnp.where(visible, scores - highest, -1e30))
    summed = jnp.sum(weights, axis=-1)
    blended = jnp.einsum(
        "hnc,cd->nhd", weights.astype(jnp.bfloat16), value_rows, preferred_element_type=jnp.float32
    )
    attended = (
        (blended / jnp.transpose(summed)[:, :, None])
        .astype(jnp.bfloat16)
        .reshape(step_rows, per_device * HD)
    )
    head_part = jnp.dot(
        attended,
        lax.all_gather(out_proj, "expert", axis=1, tiled=True),
        preferred_element_type=jnp.float32,
    )
    slot_count = tensor_count // HSPLIT
    experts = expert_count * slot_count
    most_rows = min(TOK_DEV, max(2, TOK_DEV * TOPK // experts + 1))
    capacity = tensor_count * most_rows
    slot_index = tensor_index // HSPLIT
    start_row = tensor_index * TOK_DEV
    hit_table, weight_table, rank_table, position_table = route_tables(
        expert_ids, route_weights, experts, most_rows
    )
    hit_slot = pick_slot(hit_table, expert_count, slot_count, slot_index)
    weight_slot = pick_slot(weight_table, expert_count, slot_count, slot_index)
    position_slot = pick_slot(position_table, expert_count, slot_count, slot_index)
    slot_match = (hit_slot[:, :, None] == 1) & (
        position_slot[:, :, None] == jnp.arange(capacity, dtype=jnp.int32)[None, None, :]
    )
    head_sum = lax.psum(head_part.astype(jnp.bfloat16), "tensor").astype(jnp.float32)
    residual_full = lax.all_gather(residual, "tensor", axis=0, tiled=True)
    state_full = (residual_full.astype(jnp.float32) + head_sum).astype(jnp.bfloat16)
    hidden_state = lax.dynamic_slice_in_dim(state_full, start_row, TOK_DEV, 0)
    normed_full = norm_rows(state_full, norm_gain)
    source_rows = jnp.sum(
        jnp.where(slot_match, jnp.arange(step_rows, dtype=jnp.int32)[:, None, None], 0), axis=0
    )
    filled = jnp.any(slot_match, axis=0)
    outgoing = jnp.where(
        filled[:, :, None], jnp.take(normed_full, source_rows, axis=0), jnp.zeros((), jnp.bfloat16)
    )
    arrived_rows = lax.all_to_all(outgoing, "expert", split_axis=0, concat_axis=0, tiled=True)
    flat_rows = arrived_rows.reshape(-1, arrived_rows.shape[-1])
    gate_val = jnp.dot(flat_rows, w_gate[0], preferred_element_type=jnp.float32)
    up_val = jnp.dot(flat_rows, w_up[0], preferred_element_type=jnp.float32)
    inner = (jax.nn.silu(gate_val) * up_val).astype(jnp.bfloat16)
    result = jnp.dot(inner, w_down[0], preferred_element_type=jnp.float32).astype(jnp.bfloat16)
    computed = result.reshape(arrived_rows.shape)
    returned = lax.all_to_all(computed, "expert", split_axis=0, concat_axis=0, tiled=True)
    combine_weights = jnp.where(slot_match, weight_slot[:, :, None], 0.0).astype(jnp.bfloat16)
    expert_part = jnp.einsum(
        "njc,jcd->nd", combine_weights, returned, preferred_element_type=jnp.float32
    )
    expert_share = lax.psum_scatter(
        expert_part.astype(jnp.bfloat16), "tensor", scatter_dimension=0, tiled=True
    ).astype(jnp.float32)
    return (hidden_state.astype(jnp.float32) + expert_share).astype(jnp.bfloat16)


LANES = 128
COPIES = 128


def layer_kernel(
    queries_hbm,
    cache_hbm,
    prefix_len,
    ids_hbm,
    gains_hbm,
    proj_hbm,
    residual_hbm,
    gain_hbm,
    gate_hbm,
    up_hbm,
    down_hbm,
    out,
    query,
    cached,
    bias,
    attended,
    proj,
    residual,
    gain,
    gate_up,
    down,
    ids,
    gains,
    tables,
    seen,
    heads,
    heads_sib,
    head_sum,
    heads_z,
    res_in,
    hidden,
    rows,
    part,
    part_sib,
    diag_y,
    diag_x,
    part_x,
    part_y,
    z_out,
    z_in,
    send_sem,
    recv_sem,
    load_sem,
):
    width = residual.shape[1]
    half = width // 2
    e = lax.axis_index("expert")
    t = lax.axis_index("tensor")
    x, y, z, c = e % 2, e // 2, t // 2, t % 2
    flat = [
        e,
        y * 2 + (1 - x),
        (1 - y) * 2 + x,
        (1 - y) * 2 + (1 - x),
    ]
    line = [(z + k) % 4 for k in range(4)]
    to_x, to_y, to_diag = (flat[1], t), (flat[2], t), (flat[3], t)
    to_sib = (e, z * 2 + (1 - c))
    to_z = [None] + [(e, line[k] * 2 + c) for k in range(1, 4)]

    per_device = query.shape[1] // HD
    hid = gate_hbm.shape[1]
    kv_index = t * per_device // (HEADS // KVH)
    loads = []
    for index, (source, target) in enumerate(
        (
            (cache_hbm.at[kv_index], cached),
            (queries_hbm, query),
            (residual_hbm, residual),
            (gain_hbm, gain),
            (proj_hbm, proj),
            (gate_hbm, gate_up.at[:, pl.ds(0, hid)]),
            (up_hbm, gate_up.at[:, pl.ds(hid, hid)]),
            (down_hbm, down),
            (ids_hbm, ids),
            (gains_hbm, gains),
        )
    ):
        loads.append(pltpu.make_async_copy(source, target, load_sem.at[index]))
    for index in (0, 1, 8, 9, 2, 3, 4, 5, 6, 7):
        loads[index].start()

    barrier = pltpu.get_barrier_semaphore()
    for partner in (to_x, to_y, to_diag, to_sib, *to_z[1:]):
        pl.semaphore_signal(
            barrier, inc=1, device_id=partner, device_id_type=pl.DeviceIdType.MESH
        )
    sent = []

    def send(source, target, partner):
        number = len(sent)
        copy = pltpu.make_async_remote_copy(
            src_ref=source,
            dst_ref=target,
            send_sem=send_sem.at[number],
            recv_sem=recv_sem.at[number],
            device_id=partner,
            device_id_type=pl.DeviceIdType.MESH,
        )
        copy.start()
        sent.append(copy)
        return copy

    step_rows, context = bias.shape
    columns = lax.broadcasted_iota(jnp.int32, (step_rows, context), 1)
    positions = lax.broadcasted_iota(jnp.int32, (step_rows, context), 0)
    visible = (columns < prefix_len[0]) | (columns >= PREFIX) & (columns - PREFIX <= positions)
    bias[...] = jnp.where(visible, 0.0, -1e30)

    def attend_pair(pair):
        one, two = pl.ds(2 * pair * HD, HD), pl.ds((2 * pair + 1) * HD, HD)
        stacked = jnp.concatenate([query[:, one], query[:, two]], axis=0)
        scores = lax.dot_general(
            stacked,
            cached[:, pl.ds(0, HD)],
            (((1,), (1,)), ((), ())),
            preferred_element_type=jnp.float32,
        ).reshape(2, step_rows, context)
        scores = scores + bias[...][None]
        highest = jnp.max(scores, axis=-1, keepdims=True)
        weights = jnp.exp((scores - highest) * (1.0 / math.sqrt(HD)))
        summed = jnp.sum(weights, axis=-1, keepdims=True)
        blended = jnp.dot(
            weights.astype(jnp.bfloat16).reshape(2 * step_rows, context),
            cached[:, pl.ds(HD, HD)],
            preferred_element_type=jnp.float32,
        ).reshape(2, step_rows, HD)
        blended = (blended / summed).astype(jnp.bfloat16)
        attended[:, one] = blended[0]
        attended[:, two] = blended[1]

    depth_half = attended.shape[1] // 2
    top, low = pl.ds(0, depth_half), pl.ds(depth_half, depth_half)
    loads[0].wait()
    loads[1].wait()
    for pair in range(per_device // 4):
        attend_pair(pair)
    pl.semaphore_wait(barrier, 7)
    x_top = send(attended.at[:, top], seen.at[0, :, top], to_x)
    y_top = send(attended.at[:, top], seen.at[1, :, top], to_y)
    quarter = width // 4

    def column_block(r):
        return pl.ds(pl.multiple_of(flat[r] * quarter, quarter), quarter)

    loads[2].wait()
    loads[8].wait()
    loads[9].wait()
    along_rows = lax.broadcasted_iota(jnp.int32, (LANES, step_rows), 0)
    along_lanes = lax.broadcasted_iota(jnp.int32, (LANES, step_rows), 1)
    turned = jnp.zeros((LANES, step_rows), jnp.float32)
    for place in range(TOPK):
        turned = turned + jnp.where(
            ids[place : place + 1, :] == along_rows, gains[place : place + 1, :], 0.0
        )
    unit = jnp.where(along_rows == along_lanes, 1.0, 0.0).astype(jnp.bfloat16)
    table = lax.dot_general(
        unit,
        turned.astype(jnp.bfloat16),
        (((1,), (1,)), ((), ())),
        preferred_element_type=jnp.float32,
    )
    tables[e] = table.astype(jnp.bfloat16).reshape(tables.shape[1:])
    early = []
    for r in (1, 2, 3):
        early.append(send(residual.at[:, column_block(r)], res_in.at[r], (flat[r], t)))
        early.append(send(tables.at[e], tables.at[e], (flat[r], t)))
    for pair in range(per_device // 4, per_device // 2):
        attend_pair(pair)
    y_low = send(attended.at[:, low], seen.at[1, :, low], to_y)
    x_low = send(attended.at[:, low], seen.at[0, :, low], to_x)

    def project(source, r):
        @pl.loop(0, proj.shape[1] // 256)
        def _(tile):
            columns = pl.ds(pl.multiple_of(tile * 256, 256), 256)
            value = jnp.dot(source[...], proj[:, columns], preferred_element_type=jnp.float32)
            heads[r, :, :, :, columns] = value.astype(jnp.bfloat16).reshape(4, 2, TOK_DEV, 256)

        return send(heads.at[r, :, 1 - c], heads_sib.at[r], to_sib)

    def add_cores(r, copy):
        copy.wait_recv()

        @pl.loop(0, 4)
        def _(place):
            head_sum[r, place] = (
                heads[r, place, c].astype(jnp.float32)
                + heads_sib[r, place].astype(jnp.float32)
            ).astype(jnp.bfloat16)

        return [
            send(head_sum.at[r, line[k]], heads_z.at[r, (4 - k) % 4], to_z[k])
            for k in (2, 1, 3)
        ]

    x_top.wait_recv()
    d_top = send(seen.at[0, :, top], seen.at[2, :, top], to_y)
    loads[3].wait()
    loads[4].wait()
    sib = [project(attended, 0), None, None, None]
    along = [None] * 4
    y_top.wait_recv()
    y_low.wait_recv()
    d_low = send(seen.at[1, :, low], seen.at[2, :, low], to_x)
    x_low.wait_recv()
    sib[1] = project(seen.at[0], 1)
    along[0] = add_cores(0, sib[0])
    sib[2] = project(seen.at[1], 2)
    along[1] = add_cores(1, sib[1])
    d_top.wait_recv()
    d_low.wait_recv()
    sib[3] = project(seen.at[2], 3)
    along[2] = add_cores(2, sib[2])
    along[3] = add_cores(3, sib[3])

    pairs = (y, 1 - y)
    order = (0, 1, 3, 2)
    z_rows, x_rows, y_rows, d_first, d_last = {}, {}, {}, {}, {}
    other = {}

    def state(r, place):
        for copy in along[r]:
            copy.wait_recv()
        total = head_sum[r, z].astype(jnp.float32)
        for k in range(1, 4):
            total = total + heads_z[r, k].astype(jnp.float32)
        own = residual[:, column_block(0)] if r == 0 else res_in[r]
        rows[(0, 0, 0, *place)] = (total + own.astype(jnp.float32)).astype(jnp.bfloat16)

    def launch(h):
        piece = rows.at[0, 0, 0, pairs[h]]
        for k in (2, 1, 3):
            z_rows[k, h] = send(piece, rows.at[(4 - k) % 4, 0, 0, pairs[h]], to_z[k])
        x_rows[0, h] = send(piece, rows.at[0, 1, 0, pairs[h]], to_x)
        y_rows[0, h] = send(piece, rows.at[0, 2, 0, pairs[h]], to_y)

    def share(k, r):
        other[k, r] = send(rows.at[k, r, 0], rows.at[k, r, 1], to_sib)

    def spread(k):
        for h in (0, 1):
            z_rows[(4 - k) % 4, h].wait_recv()
            piece = rows.at[k, 0, 0, pairs[h]]
            x_rows[k, h] = send(piece, rows.at[k, 1, 0, pairs[h]], to_x)
            y_rows[k, h] = send(piece, rows.at[k, 2, 0, pairs[h]], to_y)
        share(k, 0)

    def pass_on(k):
        x_rows[k, 0].wait_recv()
        d_first[k] = send(rows.at[k, 1, 0, y], rows.at[k, 3, 0, y], to_y)
        y_rows[k, 0].wait_recv()
        y_rows[k, 1].wait_recv()
        d_last[k] = send(rows.at[k, 2, 0, y], rows.at[k, 3, 0, y], to_x)
        x_rows[k, 1].wait_recv()
        share(k, 1)
        share(k, 2)

    def complete(k):
        d_first[k].wait_recv()
        d_last[k].wait_recv()
        share(k, 3)

    for copy in early:
        copy.wait_recv()
    state(0, (y, x))
    state(1, (y, 1 - x))
    launch(0)
    state(2, (1 - y, x))
    state(3, (1 - y, 1 - x))
    launch(1)
    share(0, 0)

    own_expert = e * 2 + t // HSPLIT
    slab = 8 * TOK_DEV
    half = width // 2
    front, back = pl.ds(0, half), pl.ds(half, half)
    part_copies = {}

    def experts(k):
        square = jnp.zeros((slab, 1), jnp.float32)
        both = jnp.zeros((slab, 2 * hid), jnp.float32)
        for r in range(4):
            other[k, r].wait_recv()
            values = rows[k, r].reshape(slab, quarter).astype(jnp.float32)
            square = square + jnp.sum(values * values, axis=1, keepdims=True)
            scaled = (values * gain[:, column_block(r)]).astype(jnp.bfloat16)
            both = both + jnp.dot(
                scaled, gate_up[column_block(r), :], preferred_element_type=jnp.float32
            )
        both = both * lax.rsqrt(square / width + 1e-06)
        gate_val, up_val = both[:, :hid], both[:, hid:]
        inner = (gate_val / (1.0 + jnp.exp(-gate_val)) * up_val).astype(jnp.bfloat16)
        named = lax.broadcasted_iota(jnp.int32, (slab, LANES), 1) == own_expert
        listed = jnp.concatenate(
            [tables[s, line[k] * 2 + core] for core in (c, 1 - c) for s in range(4)], axis=0
        )
        weight = jnp.sum(jnp.where(named, listed.astype(jnp.float32), 0.0), axis=1, keepdims=True)

        part_copies[k] = []
        for columns_half in (front, back):

            @pl.loop(columns_half.start // 512, (columns_half.start + half) // 512)
            def _(tile):
                columns = pl.ds(pl.multiple_of(tile * 512, 512), 512)
                value = jnp.dot(inner, down[:, columns], preferred_element_type=jnp.float32)
                part[k, :, :, :, columns] = (
                    (value * weight).astype(jnp.bfloat16).reshape(2, 4, TOK_DEV, 512)
                )

            part_copies[k].append(
                send(
                    part.at[k, 1, :, :, columns_half], part_sib.at[k, :, :, columns_half], to_sib
                )
            )

    diag_copies, plane_copies = {}, {}

    def add(k, r, columns, other_ref):
        place = (k, 0, flat[r], slice(None), columns)
        part[place] = (
            part[place].astype(jnp.float32) + other_ref.astype(jnp.float32)
        ).astype(jnp.bfloat16)

    def give_diag(k):
        diag, plane = [], []
        for copy, columns, r, diag_to, partner, plane_to in (
            (part_copies[k][0], front, 2, diag_y, to_y, part_y),
            (part_copies[k][1], back, 1, diag_x, to_x, part_x),
        ):
            copy.wait_recv()

            @pl.loop(0, 4)
            def _(s):
                part[k, 0, s, :, columns] = (
                    part[k, 0, s, :, columns].astype(jnp.float32)
                    + part_sib[k, s, :, columns].astype(jnp.float32)
                ).astype(jnp.bfloat16)

            diag.append(send(part.at[k, 0, flat[3], :, columns], diag_to.at[k], partner))
            plane.append(
                send(part.at[k, 0, flat[r], :, columns], plane_to.at[k, :, columns], partner)
            )
        diag_copies[k] = diag
        plane_copies[k] = plane

    def give_plane(k):
        from_y, from_x = diag_copies[k]
        from_y.wait_recv()
        add(k, 1, front, diag_y[k])
        plane_copies[k].append(
            send(part.at[k, 0, flat[1], :, front], part_x.at[k, :, front], to_x)
        )
        from_x.wait_recv()
        add(k, 2, back, diag_x[k])
        plane_copies[k].append(
            send(part.at[k, 0, flat[2], :, back], part_y.at[k, :, back], to_y)
        )

    z_copies = {}

    def give_line(k):
        for copy in plane_copies[k]:
            copy.wait_recv()
        total = (
            part[k, 0, e].astype(jnp.float32)
            + part_x[k].astype(jnp.float32)
            + part_y[k].astype(jnp.float32)
        )
        if k:
            z_out[k] = total.astype(jnp.bfloat16)
            z_copies[k] = send(z_out.at[k], z_in.at[(4 - k) % 4], to_z[k])
        else:
            hidden[...] = total

    a, b, f, g = order
    spread(b)
    pass_on(a)
    complete(a)
    spread(f)
    pass_on(b)
    for load in loads[5:8]:
        load.wait()
    experts(a)
    complete(b)
    spread(g)
    pass_on(f)
    experts(b)
    complete(f)
    pass_on(g)
    give_diag(b)
    experts(f)
    complete(g)
    give_plane(b)
    give_diag(f)
    experts(g)
    give_line(b)
    give_plane(f)
    give_diag(g)
    give_diag(a)
    give_line(f)
    give_plane(g)
    give_plane(a)
    give_line(g)
    give_line(a)
    total = hidden[...]
    for k in order[1:]:
        z_copies[k].wait_recv()
        total = total + z_in[(4 - k) % 4].astype(jnp.float32)
    hidden[...] = total
    for r in range(4):
        columns = column_block(r)
        out[:, columns] = (
            hidden[:, columns] + rows[0, r, 0, y, x].astype(jnp.float32)
        ).astype(jnp.bfloat16)
    for copy in sent:
        copy.wait_send()


def dense_shards(
    queries,
    keys_values,
    prefix_len,
    out_proj,
    residual,
    norm_gain,
    expert_ids,
    route_weights,
    w_gate,
    w_up,
    w_down,
):
    width = residual.shape[1]
    depth, cols = out_proj.shape
    seq = queries.shape[0]
    context = keys_values.shape[2]
    hid = w_gate.shape[2]
    bf = jnp.bfloat16
    vmem = pl.BlockSpec(memory_space=pltpu.VMEM)
    smem = pl.BlockSpec(memory_space=pltpu.SMEM)
    hbm = pl.BlockSpec(memory_space=pltpu.HBM)
    return pl.pallas_call(
        layer_kernel,
        out_shape=jax.ShapeDtypeStruct((TOK_DEV, width), bf),
        in_specs=[hbm, hbm, smem, hbm, hbm, hbm, hbm, hbm, hbm, hbm, hbm],
        out_specs=vmem,
        scratch_shapes=[
            pltpu.VMEM((seq, depth), bf),
            pltpu.VMEM((context, 2 * HD), bf),
            pltpu.VMEM((seq, context), jnp.float32),
            pltpu.VMEM((seq, depth), bf),
            pltpu.VMEM((depth, cols), bf),
            pltpu.VMEM((TOK_DEV, width), bf),
            pltpu.VMEM((1, width), jnp.float32),
            pltpu.VMEM((width, 2 * hid), bf),
            pltpu.VMEM((hid, width), bf),
            pltpu.VMEM((TOPK, seq), jnp.int32),
            pltpu.VMEM((TOPK, seq), jnp.float32),
            pltpu.VMEM((4, 8, TOK_DEV, LANES), bf),
            pltpu.VMEM((3, seq, depth), bf),
            pltpu.VMEM((4, 4, 2, TOK_DEV, cols), bf),
            pltpu.VMEM((4, 4, TOK_DEV, cols), bf),
            pltpu.VMEM((4, 4, TOK_DEV, cols), bf),
            pltpu.VMEM((4, 4, TOK_DEV, cols), bf),
            pltpu.VMEM((4, TOK_DEV, cols), bf),
            pltpu.VMEM((TOK_DEV, width), jnp.float32),
            pltpu.VMEM((4, 4, 2, 2, 2, TOK_DEV, cols), bf),
            pltpu.VMEM((4, 2, 4, TOK_DEV, width), bf),
            pltpu.VMEM((4, 4, TOK_DEV, width), bf),
            pltpu.VMEM((4, TOK_DEV, width // 2), bf),
            pltpu.VMEM((4, TOK_DEV, width // 2), bf),
            pltpu.VMEM((4, TOK_DEV, width), bf),
            pltpu.VMEM((4, TOK_DEV, width), bf),
            pltpu.VMEM((4, TOK_DEV, width), bf),
            pltpu.VMEM((4, TOK_DEV, width), bf),
            pltpu.SemaphoreType.DMA((COPIES,)),
            pltpu.SemaphoreType.DMA((COPIES,)),
            pltpu.SemaphoreType.DMA((10,)),
        ],
        compiler_params=pltpu.CompilerParams(
            collective_id=0, has_side_effects=True, vmem_limit_bytes=63 * 1024 * 1024
        ),
    )(
        queries,
        keys_values[0],
        prefix_len,
        expert_ids.T,
        route_weights.T.astype(jnp.float32),
        out_proj,
        residual,
        norm_gain[None, :],
        w_gate[0],
        w_up[0],
        w_down[0],
    )


def solution(mesh):
    experts = mesh.shape["expert"] * mesh.shape["tensor"] // HSPLIT
    dense = experts == TOPK and mesh.shape["expert"] == 4 and mesh.shape["tensor"] == 8
    return jax.shard_map(
        dense_shards if dense else shards,
        mesh=mesh,
        in_specs=(
            P("expert", "tensor"),
            P("expert", None, None, None),
            P("expert"),
            P("tensor", "expert"),
            P(("expert", "tensor"), None),
            P(),
            P("expert", None),
            P("expert", None),
            P(("expert", "tensor"), None, None),
            P(("expert", "tensor"), None, None),
            P(("expert", "tensor"), None, None),
        ),
        out_specs=P(("expert", "tensor"), None),
        check_vma=False,
    )
```
